256 devices in a mesh: blk: 64 (over y, z, core), line: 4 (over x).
Axes of the slice: x: 4, y: 4, z: 8, core: 2. Of those that a mesh axis runs over, the one named last changes fastest.
Arguments:
- field: float32 [3, 384, 512, 128], P(None, 'line', 'blk'), may hold values from -6 to 6
- stretch: float32 [384, 512, 128], P('line', 'blk'), may hold values from 0.3 to 3
- lengths: int32 [512], P('blk'), may hold values from 3 to 128, as said below
- connect: int32 [512], P('blk'), may hold values from 0 to 511, as said below
- orient: int32 [512], P('blk'), may hold values from 0 to 3
Outputs:
- rates: float32 [3, 384, 512, 128], P(None, 'line', 'blk')
- advanced: float32 [3, 384, 512, 128], P(None, 'line', 'blk')
The draws below stay inside these ranges and needn't reach their ends.
Inputs may be any that keep to these rules, and one draw needn't show every extreme that they name: `lengths`: at least 3; some slot has exactly 128. `connect`: A permutation of the slots. Slots of device d are d * 8 to d * 8 + 7. With M = 4, offset 1 = 63 and offset k = 32 + k - 2 for k from 2 to M: for each k, exactly 2 slots of every device d take their neighbours from slots of device (d + offset k) mod 64, at the same slot positions on every device.
All inputs are finite; a program needn't handle non-finite values.
Results may differ from the reference program's by a relative error of at most 0.0003.
Values sent between devices are 32-bit elements; how exact they have to be, the bound alone decides.
No kernel may reach another device: no remote copies, remote signals or barrier semaphores. Data moves between devices by JAX's collectives and lax.ppermute only.
A program may use at most 64 MiB of HBM per device.

```python
import math
import jax
import jax.numpy as jnp
from jax import lax

LINE_POINTS = 384
SLOTS_DEV = 8
NL = 128
HALO_LINES = 3
CAP = 2
SLOTS = 512
N_BLK = 64


def draw_lengths(key, part):
    key = jax.random.fold_in(key, 12)
    values = jax.random.randint(key, (N_BLK * SLOTS_DEV,), max(HALO_LINES, NL // 4), NL + 1)
    return values.at[0].set(NL).astype(jnp.int32)


def draw_connect(key, part):
    key = jax.random.fold_in(key, 11)
    key_sigma, key_pair = jax.random.split(key, 2)
    sigma = jax.random.permutation(key_sigma, SLOTS_DEV)
    shift_count = SLOTS_DEV // CAP
    kvals = jnp.arange(1, shift_count + 1)
    offsets = jnp.where(kvals == 1, N_BLK - 1, N_BLK // 2 + kvals - 2)
    slot_shift = jnp.repeat(offsets, CAP)[jax.random.permutation(key_pair, SLOTS_DEV)]
    devices = jnp.arange(N_BLK)[:, None]
    source = (devices + slot_shift[None, :]) % N_BLK
    return (source * SLOTS_DEV + sigma[None, :]).reshape(-1).astype(jnp.int32)


def plant(values, rng, low, largest):
    extent = values.shape
    spot = [jax.random.randint(jax.random.fold_in(rng, axis), (), 0, extent[axis]) for axis in range(len(extent))]
    values = values.at[tuple(spot)].set(low)
    longest = extent.index(max(extent))
    spot[longest] = (spot[longest] + 1) % extent[longest]
    return values.at[tuple(spot)].set(largest)


def block_levels(own_key, extent, shards, least, largest):
    def one(position, blocks):
        steps = jax.random.uniform(jax.random.fold_in(jax.random.fold_in(own_key, 6), position), (blocks,), jnp.float32, least / len(shards), largest / len(shards))
        return jnp.repeat(jnp.exp(steps), extent[position] // blocks).reshape((-1,) + (1,) * (len(extent) - position - 1))

    loudness = one(*shards[0])
    for cut in shards[1:]:
        loudness = loudness * one(*cut)
    return loudness


def gaussian(rng, dims, width, reach, shards=(), kind=jnp.bfloat16):
    drawn = width * jax.random.normal(rng, dims, jnp.float32)
    if shards:
        drawn = drawn * block_levels(rng, dims, shards, -0.22, 0.18)
    return jnp.clip(drawn, -reach, reach).astype(kind)


def setup_inputs(seed: int = 0) -> dict:
    seeds = jax.random.split(jax.random.key(seed), 6)
    return {
        "field": gaussian(seeds[0], (3, LINE_POINTS, SLOTS, NL), 1.0, 6.0, ((1, 4), (2, 64)), jnp.float32),
        "stretch": jnp.clip(jnp.exp(math.log(3.0) - 2.3025851 * jax.random.uniform(seeds[1], (LINE_POINTS, SLOTS, NL), jnp.float32) ** block_levels(seeds[1], (LINE_POINTS, SLOTS, NL), ((0, 4), (1, 64)), -0.2, 0.2)), 0.3, 3.0),
        "lengths": draw_lengths(jax.random.fold_in(seeds[5], 71), 0),
        "connect": draw_connect(jax.random.fold_in(seeds[5], 71), 0),
        "orient": plant(jax.random.randint(seeds[4], (SLOTS,), 0, 4), jax.random.fold_in(seeds[4], 1), 0, 3).astype(jnp.int32),
    }


stencil = (2.0, -27.0, 270.0, -490.0, 270.0, -27.0, 2.0)

def implicit_matrix(count):
    rows = jnp.arange(count)[:, None]
    cols = jnp.arange(count)[None, :]
    gap = jnp.abs(rows - cols)
    amat = jnp.where(gap == 0, 1.0, 0.0) + jnp.where(gap == 1, 2.0 / 11.0, 0.0)
    bmat = jnp.where(gap == 0, -24.0 / 11.0 - 3.0 / 22.0, 0.0) + jnp.where(gap == 1, 12.0 / 11.0, 0.0) + jnp.where(gap == 2, 3.0 / 44.0, 0.0)
    amat = amat.astype(jnp.float32)
    system = (amat - 800.0 * bmat).astype(jnp.float32)
    return jnp.linalg.solve(system, amat)

def rotate(unmasked_values, orient):
    cosine = (jnp.where(orient == 0, 1.0, 0.0) - jnp.where(orient == 2, 1.0, 0.0)).astype(jnp.float32)
    sine = (jnp.where(orient == 1, 1.0, 0.0) - jnp.where(orient == 3, 1.0, 0.0)).astype(jnp.float32)
    cosine = cosine[None, :, None]
    sine = sine[None, :, None]
    first = cosine * unmasked_values[0] - sine * unmasked_values[1]
    second = sine * unmasked_values[0] + cosine * unmasked_values[1]
    return jnp.stack([first, second, unmasked_values[2]])

def reference(field, stretch, lengths, connect, orient):
    slot_count = lengths.shape[0]
    live = (jnp.arange(NL)[None, :] < lengths[:, None]).astype(jnp.float32)
    masked_values = field * live
    position_index = lengths[:, None] - HALO_LINES + jnp.arange(HALO_LINES)[None, :]
    boundary_faces = masked_values[:, :, jnp.arange(slot_count)[:, None], position_index]
    unmasked_values = boundary_faces[:, :, connect, :]
    ghosts = rotate(unmasked_values, orient)
    trailing_rows = jnp.zeros((3, LINE_POINTS, slot_count, HALO_LINES), jnp.float32)
    ext = jnp.concatenate([ghosts, masked_values, trailing_rows], axis=3)
    second = jnp.zeros_like(masked_values)
    for shift_at in range(7):
        second = second + stencil[shift_at] * ext[:, :, :, shift_at:shift_at + NL]
    second = second / 180.0
    rates = stretch * second * live
    pre = masked_values + 0.1 * rates
    kmat = implicit_matrix(LINE_POINTS)
    advanced = jnp.einsum('pq,cqsl->cpsl', kmat, pre, precision=lax.Precision.HIGHEST)
    return (rates, advanced)
```

```python
import functools

import jax
import jax.numpy as jnp
import ml_dtypes
import numpy as np
from jax import lax
from jax.experimental import pallas as pl
from jax.experimental.pallas import tpu as pltpu
from jax.sharding import PartitionSpec as P

HALO_LINES = 3
STENCIL = (2.0, -27.0, 270.0, -490.0, 270.0, -27.0, 2.0)
SLOTS, LANES = 8, 128
GROUP = 4
PER_TILE = LANES // GROUP


def implicit_matrix(count):
    gap = np.abs(np.arange(count)[:, None] - np.arange(count)[None, :])
    amat = np.where(gap == 0, 1.0, 0.0) + np.where(gap == 1, 2.0 / 11.0, 0.0)
    bmat = (
        np.where(gap == 0, -24.0 / 11.0 - 3.0 / 22.0, 0.0)
        + np.where(gap == 1, 12.0 / 11.0, 0.0)
        + np.where(gap == 2, 3.0 / 44.0, 0.0)
    )
    return np.linalg.solve(amat - 800.0 * bmat, amat)


@functools.lru_cache(None)
def tables(count, parts):
    kmat = implicit_matrix(count)
    size = count // parts
    cut = [slice(e * size, (e + 1) * size) for e in range(parts)]
    basis = {}
    for e in range(parts):
        for side, rows in (("after", slice((e + 1) * size, count)), ("before", slice(0, e * size))):
            block = kmat[rows, cut[e]]
            if block.size:
                basis[e, side] = np.linalg.svd(block, full_matrices=False)[2][:2]
    side = lambda e, i: "after" if i > e else "before"
    project = np.zeros((parts, 4, size))
    out = np.zeros((parts, 6, size))
    for e in range(parts):
        assert side(e, e ^ 2) == side(e, e ^ 3)
        project[e, 0:2] = basis[e, side(e, e ^ 1)]
        project[e, 2:4] = basis[e, side(e, e ^ 2)]
        for k in (1, 2, 3):
            src = e ^ k
            out[e, 2 * k - 2 : 2 * k] = (kmat[cut[e], cut[src]] @ basis[src, side(src, e)].T).T
    packed = np.zeros((parts, 4, size // PER_TILE, LANES))
    for h in range(size // PER_TILE):
        packed[:, :, h] = np.repeat(project[:, :, h * PER_TILE : (h + 1) * PER_TILE], GROUP, axis=2)
    own = np.stack([np.kron(kmat[c, c], np.eye(SLOTS)) for c in cut])
    high = own.astype(ml_dtypes.bfloat16)
    low = (own - high.astype(np.float64)).astype(ml_dtypes.bfloat16)
    f32 = np.float32
    return (
        project.reshape(parts, -1).astype(f32),
        packed.astype(f32),
        out.reshape(parts, -1).astype(f32),
        high,
        low,
    )


def iota(axis):
    return lax.broadcasted_iota(jnp.int32, (SLOTS, LANES), axis)


def by_slot(ref, f=lambda v: v):
    rows = iota(0)
    tile = jnp.full((SLOTS, LANES), f(ref[0]))
    for s in range(1, SLOTS):
        tile = jnp.where(rows == s, f(ref[s]), tile)
    return tile


def faces_kernel(lengths, field, faces):
    lane = iota(1)
    source = by_slot(lengths) - HALO_LINES + jnp.minimum(lane % GROUP, HALO_LINES - 1)
    tiles = faces.shape[0] // 3
    for k in range(faces.shape[0]):
        c, h = divmod(k, tiles)
        tile = jnp.zeros((SLOTS, LANES), jnp.float32)
        for j in range(PER_TILE):
            picked = jnp.take_along_axis(
                field[c, h * PER_TILE + j], source, axis=1, mode="promise_in_bounds"
            )
            tile = jnp.where(lane // GROUP == j, picked, tile)
        faces[k] = tile


def interior_kernel(lengths, project, field, stretch, rates, coef, edge):
    part = lax.axis_index("line")
    size = field.shape[1]
    lane = iota(1)
    live = jnp.where(lane < by_slot(lengths), 1.0, 0.0).astype(jnp.float32)
    weight = []
    for k in range(7):
        from_lane = lane + (k - 3)
        inside = (from_lane >= 0) & (from_lane < LANES)
        weight.append(jnp.where(inside, STENCIL[k] / 180.0, 0.0).astype(jnp.float32))

    for h in range(size // PER_TILE):

        def step(j, carry, h=h):
            sums, tile = carry
            p = h * PER_TILE + j
            metric = stretch[p]
            tile = jnp.where(lane // GROUP == j, pltpu.roll(metric, GROUP * j, 1), tile)
            metric = metric * live
            sums = list(sums)
            for c in range(3):
                x = field[c, p] * live
                second = weight[3] * x
                for k in (0, 1, 2, 4, 5, 6):
                    second = second + weight[k] * pltpu.roll(x, (3 - k) % LANES, 1)
                rate = metric * second
                rates[c, p] = rate
                pre = x + 0.1 * rate
                for r in range(4):
                    sums[3 * r + c] = sums[3 * r + c] + project[part, r * size + p] * pre
            return tuple(sums), tile

        zero = jnp.zeros((SLOTS, LANES), jnp.float32)
        start = (zero,) * 12 if h == 0 else sums
        sums, tile = lax.fori_loop(0, PER_TILE, step, (start, zero), unroll=4)
        edge[h] = tile
    for r in range(4):
        for c in range(3):
            coef[r, c] = sums[3 * r + c]


def ghost_kernel(connect, orient, packed, chip, far, pair, swap, edge, coef, delta, near_out, far_out, rows):
    part = lax.axis_index("line")
    blk = lax.axis_index("blk")
    core = blk % 2
    lane = iota(1)
    tiles = chip.shape[0]
    parts = tiles // 3
    for k in range(tiles):
        rows[0, k] = jnp.where(core == 0, swap[k], chip[k])
        rows[1, k] = pair[k]
        rows[2, k] = jnp.where(core == 0, pair[tiles + k], swap[k])
        rows[3, k] = jnp.where(core == 0, far[k], swap[tiles + k])
    count = lax.axis_size("blk")
    raw = [jnp.zeros((SLOTS, LANES), jnp.float32)] * tiles
    slot = iota(0)
    for s in range(SLOTS):
        shift = lax.rem(connect[s] // SLOTS - blk + count, count)
        which = jnp.where(shift == count - 1, 0, shift - (count // 2 - 1))
        src = connect[s] % SLOTS
        row = rows[which, :, pl.ds(src, 1), :]
        for k in range(tiles):
            raw[k] = jnp.where(slot == s, row[k], raw[k])
    cosine = by_slot(orient, lambda k: jnp.where(k == 0, 1.0, jnp.where(k == 2, -1.0, 0.0)))
    sine = by_slot(orient, lambda k: jnp.where(k == 1, 1.0, jnp.where(k == 3, -1.0, 0.0)))
    at = lane % GROUP
    w0 = jnp.where(at < 3, STENCIL[0] / 180.0, 0.0)
    w1 = jnp.where(at < 2, STENCIL[1] / 180.0, 0.0)
    w2 = jnp.where(at < 1, STENCIL[2] / 180.0, 0.0)
    sums = [None] * 12
    for h in range(parts):
        g0 = cosine * raw[h] - sine * raw[parts + h]
        g1 = sine * raw[h] + cosine * raw[parts + h]
        for c, g in enumerate((g0, g1, raw[2 * parts + h])):
            second = w0 * g + w1 * pltpu.roll(g, LANES - 1, 1) + w2 * pltpu.roll(g, LANES - 2, 1)
            rate = edge[h] * second
            delta[c * parts + h] = rate
            for r in range(4):
                term = packed[part, r, pl.ds(h, 1), :] * rate
                i = 3 * r + c
                sums[i] = term if h == 0 else sums[i] + term
    for step in (GROUP, 2 * GROUP, 4 * GROUP, 8 * GROUP, 16 * GROUP):
        sums = [v + pltpu.roll(v, step, 1) for v in sums]
    first = jnp.where(lane < HALO_LINES, 0.1, 0.0)
    for r in range(4):
        for c in range(3):
            total = coef[r, c] + first * sums[3 * r + c]
            if r < 2:
                near_out[r, c] = total
            else:
                far_out[r - 2, c] = total


def local_kernel(lengths, field, interior, delta, high_hbm, low_hbm, rates, local, high, low, x_high, x_low, sems):
    part = lax.axis_index("line")
    copy_high = pltpu.make_async_copy(high_hbm.at[part], high, sems.at[0])
    copy_low = pltpu.make_async_copy(low_hbm.at[part], low, sems.at[1])
    copy_high.start()
    copy_low.start()
    size = field.shape[1]
    lane = iota(1)
    live = jnp.where(lane < by_slot(lengths), 1.0, 0.0).astype(jnp.float32)
    first = lane < HALO_LINES
    tiles = size // PER_TILE
    for c in range(3):
        for h in range(tiles):

            def step(j2, _, c=c, h=h):
                highs, lows = [], []
                for u in range(2):
                    j = 2 * j2 + u
                    p = h * PER_TILE + j
                    ghost = pltpu.roll(delta[c * tiles + h], lax.rem(LANES - GROUP * j, LANES), 1)
                    rate = interior[c, p] + jnp.where(first, ghost, 0.0)
                    rates[c, p] = rate
                    pre = field[c, p] * live + 0.1 * rate
                    top = pre.astype(jnp.bfloat16)
                    highs.append(top)
                    lows.append((pre - top.astype(jnp.float32)).astype(jnp.bfloat16))
                at = pl.multiple_of((h * PER_TILE + 2 * j2) * SLOTS, 2 * SLOTS)
                x_high[pl.ds(at, 2 * SLOTS), pl.ds(c * LANES, LANES)] = jnp.concatenate(highs, axis=0)
                x_low[pl.ds(at, 2 * SLOTS), pl.ds(c * LANES, LANES)] = jnp.concatenate(lows, axis=0)
                return 0

            lax.fori_loop(0, PER_TILE // 2, step, 0, unroll=4)
    copy_high.wait()
    copy_low.wait()
    dot = functools.partial(jnp.dot, preferred_element_type=jnp.float32)
    block = 128
    for b in range(size * SLOTS // block):
        rows = pl.ds(b * block, block)
        total = dot(high[rows, :], x_high[...]) + dot(high[rows, :], x_low[...]) + dot(low[rows, :], x_high[...])
        for c in range(3):
            local[c, pl.ds(b * block // SLOTS, block // SLOTS)] = total[:, c * LANES : (c + 1) * LANES].reshape(
                block // SLOTS, SLOTS, LANES
            )


def last_kernel(out, local, one, two, three, advanced):
    part = lax.axis_index("line")
    size = local.shape[1]
    for c in range(3):
        got = [ref[r, c] for ref in (one, two, three) for r in range(2)]

        def step(p, _, c=c, got=got):
            total = local[c, p]
            for k in range(6):
                total = total + out[part, k * size + p] * got[k]
            advanced[c, p] = total
            return 0

        lax.fori_loop(0, size, step, 0, unroll=8)


SMEM = pl.BlockSpec(memory_space=pltpu.SMEM)
VMEM = pl.BlockSpec(memory_space=pltpu.VMEM)
HBM = pl.BlockSpec(memory_space=pltpu.HBM)


def call(kernel, name, ins, outs, mib, flops, moved, scratch=()):
    shape = lambda s: jax.ShapeDtypeStruct(s, jnp.float32)
    return pl.pallas_call(
        kernel,
        out_shape=[shape(s) for s in outs] if isinstance(outs, list) else shape(outs),
        in_specs=ins,
        out_specs=[VMEM] * len(outs) if isinstance(outs, list) else VMEM,
        scratch_shapes=scratch,
        compiler_params=pltpu.CompilerParams(vmem_limit_bytes=mib << 20),
        cost_estimate=pl.CostEstimate(flops=flops, bytes_accessed=moved, transcendentals=0),
        name=name,
    )


def shards(field, stretch, lengths, connect, orient, *, points, parts, count):
    size = field.shape[1]
    project, packed, out, high, low = (jnp.asarray(t) for t in tables(points, parts))
    tiles = 3 * (size // PER_TILE)
    block = (3, size, SLOTS, LANES)
    packed_tile = (tiles, SLOTS, LANES)
    half = count // 2

    def over_blk(x, pairs):
        return lax.ppermute(x, "blk", pairs)

    core = [(d ^ 1, d) for d in range(count)]
    pair = [((d + half) % count, d) for d in range(count)]
    far = [((d + half + 2) % count if d % 2 == 0 else (d - 2) % count, d) for d in range(count)]

    with jax.named_scope("faces"):
        faces = call(faces_kernel, "faces", [SMEM, VMEM], packed_tile, 8, 10**6, 1200000)(lengths, field)
        chip = over_blk(faces, core)
        both = jnp.concatenate([faces, chip], axis=0)
        from_far = over_blk(both, far)
        from_pair = over_blk(both, pair)
        swapped = over_blk(from_far, core)
    with jax.named_scope("interior"):
        interior, coef, edge = call(
            interior_kernel, "interior", [SMEM, SMEM, VMEM, VMEM],
            [block, (4, 3, SLOTS, LANES), (size // PER_TILE, SLOTS, LANES)], 8, 10**7, 3000000,
        )(lengths, project, field, stretch)
    with jax.named_scope("ghosts"):
        delta, near_sum, far_sum = call(
            ghost_kernel, "ghosts", [SMEM, SMEM] + [VMEM] * 7,
            [packed_tile, (2, 3, SLOTS, LANES), (2, 3, SLOTS, LANES)], 8, 10**6, 500000,
            scratch=[pltpu.VMEM((4,) + packed_tile, jnp.float32)],
        )(connect, orient, packed, chip, from_far, from_pair, swapped, edge, coef)

    def over_line(x, k):
        return lax.ppermute(x, "line", [(e ^ k, e) for e in range(parts)])

    with jax.named_scope("line"):
        got = [over_line(near_sum, 1), over_line(far_sum, 2), over_line(far_sum, 3)]
    with jax.named_scope("local"):
        rows = size * SLOTS
        rates, local = call(
            local_kernel, "local", [SMEM, VMEM, VMEM, VMEM, HBM, HBM], [block, block], 24, 3 * 10**9, 6000000,
            scratch=[
                pltpu.VMEM((rows, rows), jnp.bfloat16),
                pltpu.VMEM((rows, rows), jnp.bfloat16),
                pltpu.VMEM((rows, 3 * LANES), jnp.bfloat16),
                pltpu.VMEM((rows, 3 * LANES), jnp.bfloat16),
                pltpu.SemaphoreType.DMA((2,)),
            ],
        )(lengths, field, interior, delta, high, low)
    with jax.named_scope("last"):
        advanced = call(last_kernel, "last", [SMEM] + [VMEM] * 4, block, 8, 10**7, 2400000)(out, local, *got)
    return rates, advanced


def solution(mesh):
    parts, count = mesh.shape["line"], mesh.shape["blk"]

    def run(field, stretch, lengths, connect, orient):
        body = functools.partial(shards, points=field.shape[1], parts=parts, count=count)
        spec = P(None, "line", "blk", None)
        return jax.shard_map(
            body,
            mesh=mesh,
            in_specs=(spec, P("line", "blk", None), P("blk"), P("blk"), P("blk")),
            out_specs=(spec, spec),
            check_vma=False,
        )(field, stretch, lengths, connect, orient)

    return run
```

```python
import functools

import jax
import jax.numpy as jnp
import ml_dtypes
import numpy as np
from jax import lax
from jax.experimental import pallas as pl
from jax.experimental.pallas import tpu as pltpu
from jax.sharding import PartitionSpec as P

HALO_LINES = 3
STENCIL = (2.0, -27.0, 270.0, -490.0, 270.0, -27.0, 2.0)
SLOTS, LANES = 8, 128
GROUP = 4
PER_TILE = LANES // GROUP


def implicit_matrix(count):
    gap = np.abs(np.arange(count)[:, None] - np.arange(count)[None, :])
    amat = np.where(gap == 0, 1.0, 0.0) + np.where(gap == 1, 2.0 / 11.0, 0.0)
    bmat = (
        np.where(gap == 0, -24.0 / 11.0 - 3.0 / 22.0, 0.0)
        + np.where(gap == 1, 12.0 / 11.0, 0.0)
        + np.where(gap == 2, 3.0 / 44.0, 0.0)
    )
    inverse = np.linalg.inv(amat - 800.0 * bmat)
    return inverse, inverse @ amat


@functools.lru_cache(None)
def tables(count, parts):
    inverse, kmat = implicit_matrix(count)
    size = count // parts
    cut = [slice(e * size, (e + 1) * size) for e in range(parts)]
    basis = {}
    for e in range(parts):
        for side, rows in (("after", slice((e + 1) * size, count)), ("before", slice(0, e * size))):
            block = kmat[rows, cut[e]]
            if block.size:
                basis[e, side] = np.linalg.svd(block, full_matrices=False)[2][:2]
    side = lambda e, i: "after" if i > e else "before"
    project = np.zeros((parts, 4, size))
    out = np.zeros((parts, 6, size))
    for e in range(parts):
        assert side(e, e ^ 2) == side(e, e ^ 3)
        project[e, 0:2] = basis[e, side(e, e ^ 1)]
        project[e, 2:4] = basis[e, side(e, e ^ 2)]
        for k in (1, 2, 3):
            src = e ^ k
            out[e, 2 * k - 2 : 2 * k] = (kmat[cut[e], cut[src]] @ basis[src, side(src, e)].T).T
    packed = np.zeros((parts, 4, size // PER_TILE, LANES))
    for h in range(size // PER_TILE):
        packed[:, :, h] = np.repeat(project[:, :, h * PER_TILE : (h + 1) * PER_TILE], GROUP, axis=2)
    rows = lambda t: np.repeat(t[..., None], LANES, axis=-1).astype(np.float32)
    forward = np.zeros((parts, 5, size + SLOTS))
    back = np.zeros((parts, 2, size))
    for e, c in enumerate(cut):
        inner, lower, pivot, upper, right = own_block(kmat, inverse, c)
        for p in range(size):
            for k, q in enumerate((p - 1, p, p + 1)):
                if 0 <= q < size:
                    forward[e, k, p + 1] = right[p, q] / pivot[p]
            for k in (1, 2):
                if p >= k:
                    forward[e, 2 + k, p + 1] = -lower[p, p - k] * pivot[p - k] / pivot[p]
                if p + k < size:
                    back[e, k - 1, p] = -upper[p, p + k]
    outer = np.stack([np.kron(t.T, np.eye(SLOTS)) for t in out])
    high, low = split(outer)
    outer = np.concatenate([high, high, low], axis=2)
    line = np.arange(LANES)
    gap = line[:, None] - line[None, :] + 3
    band = np.where((gap >= 0) & (gap <= 6), np.take(np.asarray(STENCIL), np.clip(gap, 0, 6)), 0.0)
    band = np.concatenate([band, band]).astype(ml_dtypes.bfloat16)
    return rows(project), packed.astype(np.float32), rows(forward), rows(back), outer, band


def split(x):
    high = x.astype(ml_dtypes.bfloat16)
    return high, (x - high.astype(np.float64)).astype(ml_dtypes.bfloat16)


def own_block(kmat, inverse, c):
    t = np.linalg.inv(inverse[c, c])
    right = t @ kmat[c, c]
    size = len(t)
    gap = np.abs(np.arange(size)[:, None] - np.arange(size)[None, :])
    assert np.abs(t[gap > 2]).max() < 1e-8 and np.abs(right[gap > 1]).max() < 1e-8
    t = np.where(gap > 2, 0.0, t)
    upper = t.copy()
    lower = np.eye(size)
    for p in range(size):
        for q in range(p + 1, min(p + 3, size)):
            lower[q, p] = upper[q, p] / upper[p, p]
            upper[q] -= lower[q, p] * upper[p]
    pivot = np.diag(upper).copy()
    return t, lower, pivot, upper / pivot[:, None], right


def iota(axis):
    return lax.broadcasted_iota(jnp.int32, (SLOTS, LANES), axis)


def is_live(lengths):
    return jnp.where(iota(1) < lengths[...], 1.0, 0.0).astype(jnp.float32)


def faces_kernel(lengths, field, faces, held, sems):
    lane = iota(1)
    source = lengths[...] - HALO_LINES + jnp.minimum(lane % GROUP, HALO_LINES - 1)
    tiles = faces.shape[0] // 3
    pieces = [(c, pl.ds(h * PER_TILE, PER_TILE)) for c in range(3) for h in range(tiles)]
    copies = [pltpu.make_async_copy(field.at[at], held.at[at], sems.at[k]) for k, at in enumerate(pieces)]
    for copy in copies:
        copy.start()
    for k, copy in enumerate(copies):
        copy.wait()
        c, h = divmod(k, tiles)
        tile = jnp.zeros((SLOTS, LANES), jnp.float32)
        for j in range(PER_TILE):
            picked = jnp.take_along_axis(
                held[c, h * PER_TILE + j], source, axis=1, mode="promise_in_bounds"
            )
            tile = jnp.where(lane // GROUP == j, picked, tile)
        faces[k] = tile


def interior_kernel(begin, more, *refs):
    lengths, project, band, field, stretch, *refs = refs
    before, (rates, coef, edge) = (refs[0] if more else None), refs[-3:]
    part = lax.axis_index("line")
    lane = iota(1)
    live = is_live(lengths)
    scale = live * (1.0 / 180.0)
    sums = [[None] * 3 for _ in range(4)]
    for h in range(edge.shape[0]):
        tile = jnp.zeros((SLOTS, LANES), jnp.float32)
        at = begin + h * PER_TILE
        for j in range(PER_TILE):
            tile = jnp.where(lane // GROUP == j, pltpu.roll(stretch[at + j], GROUP * j, 1), tile)
        edge[h] = tile
        for c in range(3):
            block = field[c, at : at + PER_TILE] * live
            flat = block.reshape(PER_TILE * SLOTS, LANES)
            high = flat.astype(jnp.bfloat16)
            low = (flat - high.astype(jnp.float32)).astype(jnp.bfloat16)
            second = jnp.dot(
                jnp.concatenate([high, low], axis=1), band[...], preferred_element_type=jnp.float32
            ).reshape(PER_TILE, SLOTS, LANES)
            for j in range(PER_TILE):
                rate = (stretch[at + j] * scale) * second[j]
                rates[c, h * PER_TILE + j] = rate
                pre = block[j] + 0.1 * rate
                for r in range(4):
                    term = project[part, r, at + j : at + j + 1, :] * pre
                    sums[r][c] = term if sums[r][c] is None else sums[r][c] + term
    for r in range(4):
        for c in range(3):
            coef[r, c] = sums[r][c] + before[r, c] if more else sums[r][c]


def ghost_kernel(connect, orient, packed, chip, far, pair, swap, edge_a, edge_b, coef, delta, near_out, far_out):
    part = lax.axis_index("line")
    blk = lax.axis_index("blk")
    count = lax.axis_size("blk")
    even = blk % 2 == 0
    lane = iota(1)
    tiles = chip.shape[0]
    parts = tiles // 3
    shift = (connect[...] // SLOTS - blk) & (count - 1)
    src = connect[...] % SLOTS
    is_one, is_two, is_three = shift == count // 2, shift == count // 2 + 1, shift == count // 2 + 2
    raw = []
    for k in range(tiles):
        pick = lambda v: jnp.take_along_axis(v, src, axis=0, mode="promise_in_bounds")
        row = pick(jnp.where(even, swap[k], chip[k]))
        row = jnp.where(is_one, pick(pair[k]), row)
        row = jnp.where(is_two, pick(jnp.where(even, pair[tiles + k], swap[k])), row)
        raw.append(jnp.where(is_three, pick(jnp.where(even, far[k], swap[tiles + k])), row))
    turn = orient[...]
    cosine = jnp.where(turn == 0, 1.0, jnp.where(turn == 2, -1.0, 0.0))
    sine = jnp.where(turn == 1, 1.0, jnp.where(turn == 3, -1.0, 0.0))
    at = lane % GROUP
    w0 = jnp.where(at < 3, STENCIL[0] / 180.0, 0.0)
    w1 = jnp.where(at < 2, STENCIL[1] / 180.0, 0.0)
    w2 = jnp.where(at < 1, STENCIL[2] / 180.0, 0.0)
    sums = [None] * 12
    for h in range(parts):
        g0 = cosine * raw[h] - sine * raw[parts + h]
        g1 = sine * raw[h] + cosine * raw[parts + h]
        for c, g in enumerate((g0, g1, raw[2 * parts + h])):
            second = w0 * g + w1 * pltpu.roll(g, LANES - 1, 1) + w2 * pltpu.roll(g, LANES - 2, 1)
            rate = (edge_a[h] if h < edge_a.shape[0] else edge_b[h - edge_a.shape[0]]) * second
            delta[c * parts + h] = rate
            for r in range(4):
                term = packed[part, r, h : h + 1, :] * rate
                i = 3 * r + c
                sums[i] = term if h == 0 else sums[i] + term
    for step in (GROUP, 2 * GROUP, 4 * GROUP, 8 * GROUP, 16 * GROUP):
        sums = [v + pltpu.roll(v, step, 1) for v in sums]
    first = jnp.where(lane < HALO_LINES, 0.1, 0.0)
    for r in range(4):
        for c in range(3):
            total = coef[r, c] + first * sums[3 * r + c]
            if r < 2:
                near_out[r, c] = total
            else:
                far_out[r - 2, c] = total


def local_kernel(lengths, forward, back, field, rates_a, rates_b, delta, rates, local, full, held, sems):
    part = lax.axis_index("line")
    size = field.shape[1]
    live = is_live(lengths)
    first = iota(1) < HALO_LINES
    tiles = size // PER_TILE
    zero = jnp.zeros((SLOTS, LANES), jnp.float32)
    step = 8

    def advance(p, x, state):
        weight = [forward[part, k, pl.ds(p, 1), :] for k in range(5)]
        new = []
        for c in range(3):
            x2, x1, y1, y2 = state[c]
            y = (weight[0] * x2 + weight[1] * x1 + weight[2] * x[c] + weight[4] * y2) + weight[3] * y1
            held[c, p] = y
            new.append((x1, x[c], y, y1))
        return new

    state = [(zero, zero, zero, zero)] * 3
    copies = []
    for h in range(tiles):
        ghosts = [delta[c * tiles + h] for c in range(3)]
        inner, offset = (rates_a, 0) if h * PER_TILE < rates_a.shape[1] else (rates_b, rates_a.shape[1])

        def body(i, carry, h=h, inner=inner, offset=offset):
            state, ghosts = carry
            for u in range(step):
                p = h * PER_TILE + step * i + u
                x = []
                for c in range(3):
                    ghost = ghosts[c] if u == 0 else pltpu.roll(ghosts[c], LANES - GROUP * u, 1)
                    rate = inner[c, p - offset] + jnp.where(first, ghost, 0.0)
                    full[c, p] = rate
                    x.append(field[c, p] * live + 0.1 * rate)
                state = advance(p, x, state)
            return state, [pltpu.roll(g, LANES - GROUP * step, 1) for g in ghosts]

        state, _ = lax.fori_loop(0, PER_TILE // step, body, (state, ghosts))
        at = (slice(None), pl.ds(h * PER_TILE, PER_TILE))
        copies.append(pltpu.make_async_copy(full.at[at], rates.at[at], sems.at[h]))
        copies[-1].start()
    state = advance(size, [zero] * 3, state)

    def descend(i, carry):
        new = list(carry)
        for u in range(step):
            p = size - 1 - (step * i + u)
            one, two = back[part, 0, pl.ds(p, 1), :], back[part, 1, pl.ds(p, 1), :]
            for c in range(3):
                z1, z2 = new[c]
                z = (held[c, p + 1] + two * z2) + one * z1
                local[c, p] = z
                new[c] = (z, z1)
        return new

    lax.fori_loop(0, size // step, descend, [(zero, zero)] * 3)
    for copy in copies:
        copy.wait()


def last_kernel(outer, local, one, two, three, advanced, full, sems):
    part = lax.axis_index("line")
    size = local.shape[1]
    got = jnp.concatenate(
        [jnp.concatenate([ref[r, c] for c in range(3)], axis=1) for ref in (one, two, three) for r in range(2)], axis=0
    )
    high = got.astype(jnp.bfloat16)
    low = (got - high.astype(jnp.float32)).astype(jnp.bfloat16)
    got = jnp.concatenate([high, low, high], axis=0)
    copies = []
    for h in range(size // PER_TILE):
        rows = slice(h * PER_TILE * SLOTS, (h + 1) * PER_TILE * SLOTS)
        total = jnp.dot(outer[part, rows, :], got, preferred_element_type=jnp.float32)
        at = pl.ds(h * PER_TILE, PER_TILE)
        for c in range(3):
            tile = total[:, c * LANES : (c + 1) * LANES].reshape(PER_TILE, SLOTS, LANES)
            full[c, at] = local[c, at] + tile
            copies.append(pltpu.make_async_copy(full.at[c, at], advanced.at[c, at], sems.at[3 * h + c]))
            copies[-1].start()
    for copy in copies:
        copy.wait()


SMEM = pl.BlockSpec(memory_space=pltpu.SMEM)
VMEM = pl.BlockSpec(memory_space=pltpu.VMEM)
HBM = pl.BlockSpec(memory_space=pltpu.HBM)


def call(kernel, name, ins, outs, mib, flops, moved, scratch=(), out_specs=None):
    shape = lambda s: jax.ShapeDtypeStruct(s, jnp.float32)
    return pl.pallas_call(
        kernel,
        out_shape=[shape(s) for s in outs],
        in_specs=ins,
        out_specs=out_specs or [VMEM] * len(outs),
        scratch_shapes=scratch,
        compiler_params=pltpu.CompilerParams(vmem_limit_bytes=mib << 20),
        cost_estimate=pl.CostEstimate(flops=flops, bytes_accessed=moved, transcendentals=0),
        name=name,
    )


def shards(field, stretch, lengths, connect, orient, *, points, parts, count):
    size = field.shape[1]
    project, packed, forward, back, outer, band = (jnp.asarray(t) for t in tables(points, parts))
    tiles = 3 * (size // PER_TILE)
    block = (3, size, SLOTS, LANES)
    packed_tile = (tiles, SLOTS, LANES)
    sums = (4, 3, SLOTS, LANES)
    half = count // 2
    lengths, connect, orient = (jnp.broadcast_to(v[:, None], (SLOTS, LANES)) for v in (lengths, connect, orient))
    dma = pltpu.SemaphoreType.DMA

    def over_blk(x, pairs):
        return lax.ppermute(x, "blk", pairs)

    core = [(d ^ 1, d) for d in range(count)]
    pair = [((d + half) % count, d) for d in range(count)]
    far = [((d + half + 2) % count if d % 2 == 0 else (d - 2) % count, d) for d in range(count)]

    field = pltpu.with_memory_space_constraint(field, pltpu.HBM)
    with jax.named_scope("faces"):
        faces, held = call(
            faces_kernel, "faces", [VMEM, HBM], [packed_tile, block], 8, 10**6, 1200000, scratch=[dma((tiles,))]
        )(lengths, field)
        chip = over_blk(faces, core)

    def inside(begin, length, metric, *before):
        return call(
            functools.partial(interior_kernel, begin, bool(before)), "interior", [VMEM] * (5 + len(before)),
            [(3, length, SLOTS, LANES), sums, (length // PER_TILE, SLOTS, LANES)], 8, 10**7, 1500000,
        )(lengths, project, band, held, metric, *before)

    with jax.named_scope("interior"):
        rates_a, coef, edge_a = inside(0, PER_TILE, stretch)
        chip, rates_a, coef, edge_a = lax.optimization_barrier((chip, rates_a, coef, edge_a))
    with jax.named_scope("faces"):
        both = jnp.concatenate([faces, chip], axis=0)
        from_far = over_blk(both, far)
        from_pair = over_blk(both, pair)
        from_far, coef = lax.optimization_barrier((from_far, coef))
        swapped = over_blk(from_far, core)
    with jax.named_scope("interior"):
        rates_b, coef, edge_b = inside(PER_TILE, size - PER_TILE, stretch, coef)
    with jax.named_scope("ghosts"):
        delta, near_sum, far_sum = call(
            ghost_kernel, "ghosts", [VMEM] * 10,
            [packed_tile, (2, 3, SLOTS, LANES), (2, 3, SLOTS, LANES)], 8, 10**6, 500000,
        )(connect, orient, packed, chip, from_far, from_pair, swapped, edge_a, edge_b, coef)

    def over_line(x, k):
        return lax.ppermute(x, "line", [(e ^ k, e) for e in range(parts)])

    with jax.named_scope("line"):
        got = [over_line(near_sum, 1), over_line(far_sum, 2), over_line(far_sum, 3)]
    with jax.named_scope("local"):
        rates, local = call(
            local_kernel, "local", [VMEM] * 7, [block, block], 12, 10**8, 6000000,
            out_specs=[HBM, VMEM],
            scratch=[
                pltpu.VMEM(block, jnp.float32),
                pltpu.VMEM((3, size + 1, SLOTS, LANES), jnp.float32),
                dma((size // PER_TILE,)),
            ],
        )(lengths, forward, back, held, rates_a, rates_b, delta)
    with jax.named_scope("last"):
        (advanced,) = call(
            last_kernel, "last", [VMEM] * 5, [block], 8, 10**7, 2400000, out_specs=[HBM],
            scratch=[pltpu.VMEM(block, jnp.float32), dma((tiles,))],
        )(outer, local, *got)
    return rates, advanced


def solution(mesh):
    parts, count = mesh.shape["line"], mesh.shape["blk"]

    def run(field, stretch, lengths, connect, orient):
        body = functools.partial(shards, points=field.shape[1], parts=parts, count=count)
        spec = P(None, "line", "blk", None)
        return jax.shard_map(
            body,
            mesh=mesh,
            in_specs=(spec, P("line", "blk", None), P("blk"), P("blk"), P("blk")),
            out_specs=(spec, spec),
            check_vma=False,
        )(field, stretch, lengths, connect, orient)

    return run
```

```python
import functools

import jax
import jax.numpy as jnp
import ml_dtypes
import numpy as np
from jax import lax
from jax.experimental import pallas as pl
from jax.experimental.pallas import tpu as pltpu
from jax.sharding import PartitionSpec as P

HALO_LINES = 3
STENCIL = (2.0, -27.0, 270.0, -490.0, 270.0, -27.0, 2.0)
SLOTS, LANES = 8, 128
GROUP = 4
PER_TILE = LANES // GROUP


def implicit_matrix(count):
    gap = np.abs(np.arange(count)[:, None] - np.arange(count)[None, :])
    amat = np.where(gap == 0, 1.0, 0.0) + np.where(gap == 1, 2.0 / 11.0, 0.0)
    bmat = (
        np.where(gap == 0, -24.0 / 11.0 - 3.0 / 22.0, 0.0)
        + np.where(gap == 1, 12.0 / 11.0, 0.0)
        + np.where(gap == 2, 3.0 / 44.0, 0.0)
    )
    inverse = np.linalg.inv(amat - 800.0 * bmat)
    return inverse, inverse @ amat


@functools.lru_cache(None)
def tables(count, parts):
    inverse, kmat = implicit_matrix(count)
    size = count // parts
    cut = [slice(e * size, (e + 1) * size) for e in range(parts)]
    basis = {}
    for e in range(parts):
        for side, rows in (("after", slice((e + 1) * size, count)), ("before", slice(0, e * size))):
            block = kmat[rows, cut[e]]
            if block.size:
                basis[e, side] = np.linalg.svd(block, full_matrices=False)[2][:2]
    side = lambda e, i: "after" if i > e else "before"
    project = np.zeros((parts, 4, size))
    out = np.zeros((parts, 6, size))
    for e in range(parts):
        assert side(e, e ^ 2) == side(e, e ^ 3)
        project[e, 0:2] = basis[e, side(e, e ^ 1)]
        project[e, 2:4] = basis[e, side(e, e ^ 2)]
        for k in (1, 2, 3):
            src = e ^ k
            out[e, 2 * k - 2 : 2 * k] = (kmat[cut[e], cut[src]] @ basis[src, side(src, e)].T).T
    packed = np.zeros((parts, 4, size // PER_TILE, LANES))
    for h in range(size // PER_TILE):
        packed[:, :, h] = np.repeat(project[:, :, h * PER_TILE : (h + 1) * PER_TILE], GROUP, axis=2)
    rows = lambda t: np.repeat(t[..., None], LANES, axis=-1).astype(np.float32)
    forward = np.zeros((parts, 5, size + SLOTS))
    back = np.zeros((parts, 2, size))
    for e, c in enumerate(cut):
        inner, lower, pivot, upper, right = own_block(kmat, inverse, c)
        for p in range(size):
            for k, q in enumerate((p - 1, p, p + 1)):
                if 0 <= q < size:
                    forward[e, k, p + 1] = right[p, q] / pivot[p]
            for k in (1, 2):
                if p >= k:
                    forward[e, 2 + k, p + 1] = -lower[p, p - k] * pivot[p - k] / pivot[p]
                if p + k < size:
                    back[e, k - 1, p] = -upper[p, p + k]
    outer = np.stack([np.kron(t.T, np.eye(SLOTS)) for t in out])
    high, low = split(outer)
    outer = np.concatenate([high, high, low], axis=2)
    line = np.arange(LANES)
    gap = line[:, None] - line[None, :] + 3
    band = np.where((gap >= 0) & (gap <= 6), np.take(np.asarray(STENCIL), np.clip(gap, 0, 6)), 0.0)
    band = np.concatenate([band, band]).astype(ml_dtypes.bfloat16)
    return rows(project), packed.astype(np.float32), rows(forward), rows(back), outer, band


def split(x):
    high = x.astype(ml_dtypes.bfloat16)
    return high, (x - high.astype(np.float64)).astype(ml_dtypes.bfloat16)


def own_block(kmat, inverse, c):
    t = np.linalg.inv(inverse[c, c])
    right = t @ kmat[c, c]
    size = len(t)
    gap = np.abs(np.arange(size)[:, None] - np.arange(size)[None, :])
    assert np.abs(t[gap > 2]).max() < 1e-8 and np.abs(right[gap > 1]).max() < 1e-8
    t = np.where(gap > 2, 0.0, t)
    upper = t.copy()
    lower = np.eye(size)
    for p in range(size):
        for q in range(p + 1, min(p + 3, size)):
            lower[q, p] = upper[q, p] / upper[p, p]
            upper[q] -= lower[q, p] * upper[p]
    pivot = np.diag(upper).copy()
    return t, lower, pivot, upper / pivot[:, None], right


def iota(axis):
    return lax.broadcasted_iota(jnp.int32, (SLOTS, LANES), axis)


def is_live(slots):
    return jnp.where(iota(1) < slots[0], 1.0, 0.0).astype(jnp.float32)


def by_slot(ref):
    shape = (SLOTS, SLOTS)
    own = lax.broadcasted_iota(jnp.int32, shape, 0) == lax.broadcasted_iota(jnp.int32, shape, 1)
    spread = jnp.where(own, jnp.broadcast_to(ref[...], shape).astype(jnp.float32), 0.0)
    return jnp.broadcast_to(jnp.sum(spread, axis=1, keepdims=True), (SLOTS, LANES)).astype(jnp.int32)


def faces_kernel(lengths, connect, orient, field, faces, held, slots, near, link, turn, sems):
    lane = iota(1)
    tiles = faces.shape[0] // 3
    pieces = [(c, pl.ds(h * PER_TILE, PER_TILE)) for c in range(3) for h in range(tiles)]
    small = [
        pltpu.make_async_copy(ref, to, sems.at[len(pieces) + k])
        for k, (ref, to) in enumerate(((lengths, near), (connect, link), (orient, turn)))
    ]
    copies = [pltpu.make_async_copy(field.at[at], held.at[at], sems.at[k]) for k, at in enumerate(pieces)]
    for copy in small + copies:
        copy.start()
    for copy in small:
        copy.wait()
    for k, ref in enumerate((near, link, turn)):
        slots[k] = by_slot(ref)
    source = slots[0] - HALO_LINES + jnp.minimum(lane % GROUP, HALO_LINES - 1)
    for k, copy in enumerate(copies):
        copy.wait()
        c, h = divmod(k, tiles)
        tile = jnp.zeros((SLOTS, LANES), jnp.float32)
        for j in range(PER_TILE):
            picked = jnp.take_along_axis(
                held[c, h * PER_TILE + j], source, axis=1, mode="promise_in_bounds"
            )
            tile = jnp.where(lane // GROUP == j, picked, tile)
        faces[k] = tile


def interior_kernel(begin, more, *refs):
    slots, project, band, field, stretch, *refs = refs
    before, (rates, coef, edge) = (refs[0] if more else None), refs[-3:]
    part = lax.axis_index("line")
    lane = iota(1)
    live = is_live(slots)
    scale = live * (1.0 / 180.0)
    sums = [[None] * 3 for _ in range(4)]
    for h in range(edge.shape[0]):
        tile = jnp.zeros((SLOTS, LANES), jnp.float32)
        at = begin + h * PER_TILE
        for j in range(PER_TILE):
            tile = jnp.where(lane // GROUP == j, pltpu.roll(stretch[at + j], GROUP * j, 1), tile)
        edge[h] = tile
        for c in range(3):
            block = field[c, at : at + PER_TILE] * live
            flat = block.reshape(PER_TILE * SLOTS, LANES)
            high = flat.astype(jnp.bfloat16)
            low = (flat - high.astype(jnp.float32)).astype(jnp.bfloat16)
            second = jnp.dot(
                jnp.concatenate([high, low], axis=1), band[...], preferred_element_type=jnp.float32
            ).reshape(PER_TILE, SLOTS, LANES)
            for j in range(PER_TILE):
                rate = (stretch[at + j] * scale) * second[j]
                rates[c, h * PER_TILE + j] = rate
                pre = block[j] + 0.1 * rate
                for r in range(4):
                    term = project[part, r, at + j : at + j + 1, :] * pre
                    sums[r][c] = term if sums[r][c] is None else sums[r][c] + term
    for r in range(4):
        for c in range(3):
            coef[r, c] = sums[r][c] + before[r, c] if more else sums[r][c]


def ghost_kernel(slots, packed, chip, far, pair, swap, edge_a, edge_b, coef, delta, near_out, far_out):
    part = lax.axis_index("line")
    blk = lax.axis_index("blk")
    count = lax.axis_size("blk")
    even = blk % 2 == 0
    lane = iota(1)
    tiles = chip.shape[0]
    parts = tiles // 3
    shift = (slots[1] // SLOTS - blk) & (count - 1)
    src = slots[1] % SLOTS
    is_one, is_two, is_three = shift == count // 2, shift == count // 2 + 1, shift == count // 2 + 2
    raw = []
    for k in range(tiles):
        pick = lambda v: jnp.take_along_axis(v, src, axis=0, mode="promise_in_bounds")
        row = pick(jnp.where(even, swap[k], chip[k]))
        row = jnp.where(is_one, pick(jnp.where(even, swap[2 * tiles + k], pair[k])), row)
        row = jnp.where(is_two, pick(jnp.where(even, swap[tiles + k], swap[k])), row)
        raw.append(jnp.where(is_three, pick(jnp.where(even, far[k], swap[tiles + k])), row))
    turn = slots[2]
    cosine = jnp.where(turn == 0, 1.0, jnp.where(turn == 2, -1.0, 0.0))
    sine = jnp.where(turn == 1, 1.0, jnp.where(turn == 3, -1.0, 0.0))
    at = lane % GROUP
    w0 = jnp.where(at < 3, STENCIL[0] / 180.0, 0.0)
    w1 = jnp.where(at < 2, STENCIL[1] / 180.0, 0.0)
    w2 = jnp.where(at < 1, STENCIL[2] / 180.0, 0.0)
    sums = [None] * 12
    for h in range(parts):
        g0 = cosine * raw[h] - sine * raw[parts + h]
        g1 = sine * raw[h] + cosine * raw[parts + h]
        for c, g in enumerate((g0, g1, raw[2 * parts + h])):
            second = w0 * g + w1 * pltpu.roll(g, LANES - 1, 1) + w2 * pltpu.roll(g, LANES - 2, 1)
            rate = (edge_a[h] if h < edge_a.shape[0] else edge_b[h - edge_a.shape[0]]) * second
            delta[c * parts + h] = rate
            for r in range(4):
                term = packed[part, r, h : h + 1, :] * rate
                i = 3 * r + c
                sums[i] = term if h == 0 else sums[i] + term
    for step in (GROUP, 2 * GROUP, 4 * GROUP, 8 * GROUP, 16 * GROUP):
        sums = [v + pltpu.roll(v, step, 1) for v in sums]
    first = jnp.where(lane < HALO_LINES, 0.1, 0.0)
    for r in range(4):
        for c in range(3):
            total = coef[r, c] + first * sums[3 * r + c]
            if r < 2:
                near_out[r, c] = total
            else:
                far_out[r - 2, c] = total


def local_kernel(slots, forward, back, field, rates_a, rates_b, delta, rates, local, full, held, sems):
    part = lax.axis_index("line")
    size = field.shape[1]
    live = is_live(slots)
    first = iota(1) < HALO_LINES
    tiles = size // PER_TILE
    zero = jnp.zeros((SLOTS, LANES), jnp.float32)
    step = 8

    def advance(p, x, state):
        weight = [forward[part, k, pl.ds(p, 1), :] for k in range(5)]
        new = []
        for c in range(3):
            x2, x1, y1, y2 = state[c]
            y = (weight[0] * x2 + weight[1] * x1 + weight[2] * x[c] + weight[4] * y2) + weight[3] * y1
            held[c, p] = y
            new.append((x1, x[c], y, y1))
        return new

    state = [(zero, zero, zero, zero)] * 3
    copies = []
    for h in range(tiles):
        ghosts = [delta[c * tiles + h] for c in range(3)]
        inner, offset = (rates_a, 0) if h * PER_TILE < rates_a.shape[1] else (rates_b, rates_a.shape[1])

        def body(i, carry, h=h, inner=inner, offset=offset):
            state, ghosts = carry
            for u in range(step):
                p = h * PER_TILE + step * i + u
                x = []
                for c in range(3):
                    ghost = ghosts[c] if u == 0 else pltpu.roll(ghosts[c], LANES - GROUP * u, 1)
                    rate = inner[c, p - offset] + jnp.where(first, ghost, 0.0)
                    full[c, p] = rate
                    x.append(field[c, p] * live + 0.1 * rate)
                state = advance(p, x, state)
            return state, [pltpu.roll(g, LANES - GROUP * step, 1) for g in ghosts]

        state, _ = lax.fori_loop(0, PER_TILE // step, body, (state, ghosts))
        at = (slice(None), pl.ds(h * PER_TILE, PER_TILE))
        copies.append(pltpu.make_async_copy(full.at[at], rates.at[at], sems.at[h]))
        copies[-1].start()
    state = advance(size, [zero] * 3, state)

    def descend(i, carry):
        new = list(carry)
        for u in range(step):
            p = size - 1 - (step * i + u)
            one, two = back[part, 0, pl.ds(p, 1), :], back[part, 1, pl.ds(p, 1), :]
            for c in range(3):
                z1, z2 = new[c]
                z = (held[c, p + 1] + two * z2) + one * z1
                local[c, p] = z
                new[c] = (z, z1)
        return new

    lax.fori_loop(0, size // step, descend, [(zero, zero)] * 3)
    for copy in copies:
        copy.wait()


def last_kernel(outer, local, one, two, three, advanced, full, sems):
    part = lax.axis_index("line")
    size = local.shape[1]
    got = jnp.concatenate(
        [jnp.concatenate([ref[r, c] for c in range(3)], axis=1) for ref in (one, two, three) for r in range(2)], axis=0
    )
    high = got.astype(jnp.bfloat16)
    low = (got - high.astype(jnp.float32)).astype(jnp.bfloat16)
    got = jnp.concatenate([high, low, high], axis=0)
    copies = []
    for h in range(size // PER_TILE):
        rows = slice(h * PER_TILE * SLOTS, (h + 1) * PER_TILE * SLOTS)
        total = jnp.dot(outer[part, rows, :], got, preferred_element_type=jnp.float32)
        at = pl.ds(h * PER_TILE, PER_TILE)
        for c in range(3):
            tile = total[:, c * LANES : (c + 1) * LANES].reshape(PER_TILE, SLOTS, LANES)
            full[c, at] = local[c, at] + tile
            copies.append(pltpu.make_async_copy(full.at[c, at], advanced.at[c, at], sems.at[3 * h + c]))
            copies[-1].start()
    for copy in copies:
        copy.wait()


SMEM = pl.BlockSpec(memory_space=pltpu.SMEM)
VMEM = pl.BlockSpec(memory_space=pltpu.VMEM)
HBM = pl.BlockSpec(memory_space=pltpu.HBM)


def call(kernel, name, ins, outs, mib, flops, moved, scratch=(), out_specs=None, kinds={}):
    return pl.pallas_call(
        kernel,
        out_shape=[jax.ShapeDtypeStruct(s, kinds.get(k, jnp.float32)) for k, s in enumerate(outs)],
        in_specs=ins,
        out_specs=out_specs or [VMEM] * len(outs),
        scratch_shapes=scratch,
        compiler_params=pltpu.CompilerParams(vmem_limit_bytes=mib << 20),
        cost_estimate=pl.CostEstimate(flops=flops, bytes_accessed=moved, transcendentals=0),
        name=name,
    )


def shards(field, stretch, lengths, connect, orient, *, points, parts, count):
    size = field.shape[1]
    project, packed, forward, back, outer, band = (jnp.asarray(t) for t in tables(points, parts))
    tiles = 3 * (size // PER_TILE)
    block = (3, size, SLOTS, LANES)
    packed_tile = (tiles, SLOTS, LANES)
    sums = (4, 3, SLOTS, LANES)
    half = count // 2
    dma = pltpu.SemaphoreType.DMA

    def over_blk(x, pairs):
        return lax.ppermute(x, "blk", pairs)

    core = [(d ^ 1, d) for d in range(count)]
    pair = [(d if d % 2 == 0 else (d + half) % count, d) for d in range(count)]
    far = [((d + half + 2) % count if d % 2 == 0 else (d - 2) % count, d) for d in range(count)]

    lengths, connect, orient = (v[None] for v in (lengths, connect, orient))
    field, lengths, connect, orient = (
        pltpu.with_memory_space_constraint(v, pltpu.HBM) for v in (field, lengths, connect, orient)
    )
    with jax.named_scope("faces"):
        faces, held, slots = call(
            faces_kernel, "faces", [HBM] * 4, [packed_tile, block, (3, SLOTS, LANES)], 8, 10**6, 1200000,
            scratch=[pltpu.VMEM((1, SLOTS), jnp.int32)] * 3 + [dma((tiles + 3,))], kinds={2: jnp.int32},
        )(lengths, connect, orient, field)
        chip = over_blk(faces, core)

    def inside(begin, length, metric, *before):
        return call(
            functools.partial(interior_kernel, begin, bool(before)), "interior", [VMEM] * (5 + len(before)),
            [(3, length, SLOTS, LANES), sums, (length // PER_TILE, SLOTS, LANES)], 8, 10**7, 1500000,
        )(slots, project, band, held, metric, *before)

    with jax.named_scope("interior"):
        rates_a, coef, edge_a = inside(0, PER_TILE, stretch)
        chip, rates_a, coef, edge_a = lax.optimization_barrier((chip, rates_a, coef, edge_a))
    with jax.named_scope("faces"):
        both = jnp.concatenate([faces, chip], axis=0)
        from_far = over_blk(both, far)
        from_pair = over_blk(both, pair)
        from_far, coef = lax.optimization_barrier((from_far, coef))
        middle = jnp.where(lax.axis_index("blk") % 2 == 0, from_far[tiles:], from_pair[:tiles])
        swapped = over_blk(jnp.concatenate([from_far[:tiles], middle, from_pair[tiles:]], axis=0), core)
    with jax.named_scope("interior"):
        rates_b, coef, edge_b = inside(PER_TILE, size - PER_TILE, stretch, coef)
    with jax.named_scope("ghosts"):
        delta, near_sum, far_sum = call(
            ghost_kernel, "ghosts", [VMEM] * 9,
            [packed_tile, (2, 3, SLOTS, LANES), (2, 3, SLOTS, LANES)], 8, 10**6, 500000,
        )(slots, packed, chip, from_far, from_pair, swapped, edge_a, edge_b, coef)

    def over_line(x, k):
        return lax.ppermute(x, "line", [(e ^ k, e) for e in range(parts)])

    with jax.named_scope("line"):
        got = [over_line(near_sum, 1), over_line(far_sum, 2), over_line(far_sum, 3)]
    with jax.named_scope("local"):
        rates, local = call(
            local_kernel, "local", [VMEM] * 7, [block, block], 12, 10**8, 6000000,
            out_specs=[HBM, VMEM],
            scratch=[
                pltpu.VMEM(block, jnp.float32),
                pltpu.VMEM((3, size + 1, SLOTS, LANES), jnp.float32),
                dma((size // PER_TILE,)),
            ],
        )(slots, forward, back, held, rates_a, rates_b, delta)
    with jax.named_scope("last"):
        (advanced,) = call(
            last_kernel, "last", [VMEM] * 5, [block], 8, 10**7, 2400000, out_specs=[HBM],
            scratch=[pltpu.VMEM(block, jnp.float32), dma((tiles,))],
        )(outer, local, *got)
    return rates, advanced


def solution(mesh):
    parts, count = mesh.shape["line"], mesh.shape["blk"]

    def run(field, stretch, lengths, connect, orient):
        body = functools.partial(shards, points=field.shape[1], parts=parts, count=count)
        spec = P(None, "line", "blk", None)
        return jax.shard_map(
            body,
            mesh=mesh,
            in_specs=(spec, P("line", "blk", None), P("blk"), P("blk"), P("blk")),
            out_specs=(spec, spec),
            check_vma=False,
        )(field, stretch, lengths, connect, orient)

    return run
```

```python
import functools

import jax
import jax.numpy as jnp
import ml_dtypes
import numpy as np
from jax import lax
from jax.experimental import pallas as pl
from jax.experimental.pallas import tpu as pltpu
from jax.sharding import PartitionSpec as P

HALO_LINES = 3
STENCIL = (2.0, -27.0, 270.0, -490.0, 270.0, -27.0, 2.0)
SLOTS, LANES = 8, 128
GROUP = 4
PER_TILE = LANES // GROUP


def implicit_matrix(count):
    gap = np.abs(np.arange(count)[:, None] - np.arange(count)[None, :])
    amat = np.where(gap == 0, 1.0, 0.0) + np.where(gap == 1, 2.0 / 11.0, 0.0)
    bmat = (
        np.where(gap == 0, -24.0 / 11.0 - 3.0 / 22.0, 0.0)
        + np.where(gap == 1, 12.0 / 11.0, 0.0)
        + np.where(gap == 2, 3.0 / 44.0, 0.0)
    )
    inverse = np.linalg.inv(amat - 800.0 * bmat)
    return inverse, inverse @ amat


@functools.lru_cache(None)
def tables(count, parts):
    inverse, kmat = implicit_matrix(count)
    size = count // parts
    cut = [slice(e * size, (e + 1) * size) for e in range(parts)]
    basis = {}
    for e in range(parts):
        for side, rows in (("after", slice((e + 1) * size, count)), ("before", slice(0, e * size))):
            block = kmat[rows, cut[e]]
            if block.size:
                basis[e, side] = np.linalg.svd(block, full_matrices=False)[2][:2]
    side = lambda e, i: "after" if i > e else "before"
    project = np.zeros((parts, 4, size))
    out = np.zeros((parts, 6, size))
    for e in range(parts):
        assert side(e, e ^ 2) == side(e, e ^ 3)
        project[e, 0:2] = basis[e, side(e, e ^ 1)]
        project[e, 2:4] = basis[e, side(e, e ^ 2)]
        for k in (1, 2, 3):
            src = e ^ k
            out[e, 2 * k - 2 : 2 * k] = (kmat[cut[e], cut[src]] @ basis[src, side(src, e)].T).T
    packed = np.zeros((parts, 4, size // PER_TILE, LANES))
    for h in range(size // PER_TILE):
        packed[:, :, h] = np.repeat(project[:, :, h * PER_TILE : (h + 1) * PER_TILE], GROUP, axis=2)
    rows = lambda t: np.repeat(t[..., None], LANES, axis=-1).astype(np.float32)
    forward = np.zeros((parts, 5, size + SLOTS))
    back = np.zeros((parts, 2, size))
    for e, c in enumerate(cut):
        inner, lower, pivot, upper, right = own_block(kmat, inverse, c)
        for p in range(size):
            for k, q in enumerate((p - 1, p, p + 1)):
                if 0 <= q < size:
                    forward[e, k, p + 1] = right[p, q] / pivot[p]
            for k in (1, 2):
                if p >= k:
                    forward[e, 2 + k, p + 1] = -lower[p, p - k] * pivot[p - k] / pivot[p]
                if p + k < size:
                    back[e, k - 1, p] = -upper[p, p + k]
    outer = np.stack([np.kron(t.T, np.eye(SLOTS)) for t in out])
    high, low = split(outer)
    outer = np.concatenate([high, high, low], axis=2)
    line = np.arange(LANES)
    gap = line[:, None] - line[None, :] + 3
    band = np.where((gap >= 0) & (gap <= 6), np.take(np.asarray(STENCIL), np.clip(gap, 0, 6)), 0.0)
    band = np.concatenate([band, band]).astype(ml_dtypes.bfloat16)
    return rows(project), packed.astype(np.float32), rows(forward), rows(back), outer, band


def split(x):
    high = x.astype(ml_dtypes.bfloat16)
    return high, (x - high.astype(np.float64)).astype(ml_dtypes.bfloat16)


def own_block(kmat, inverse, c):
    t = np.linalg.inv(inverse[c, c])
    right = t @ kmat[c, c]
    size = len(t)
    gap = np.abs(np.arange(size)[:, None] - np.arange(size)[None, :])
    assert np.abs(t[gap > 2]).max() < 1e-8 and np.abs(right[gap > 1]).max() < 1e-8
    t = np.where(gap > 2, 0.0, t)
    upper = t.copy()
    lower = np.eye(size)
    for p in range(size):
        for q in range(p + 1, min(p + 3, size)):
            lower[q, p] = upper[q, p] / upper[p, p]
            upper[q] -= lower[q, p] * upper[p]
    pivot = np.diag(upper).copy()
    return t, lower, pivot, upper / pivot[:, None], right


def iota(axis):
    return lax.broadcasted_iota(jnp.int32, (SLOTS, LANES), axis)


def is_live(slots):
    return jnp.where(iota(1) < slots[0], 1.0, 0.0).astype(jnp.float32)


def by_slot(ref):
    shape = (SLOTS, SLOTS)
    own = lax.broadcasted_iota(jnp.int32, shape, 0) == lax.broadcasted_iota(jnp.int32, shape, 1)
    spread = jnp.where(own, jnp.broadcast_to(ref[...], shape).astype(jnp.float32), 0.0)
    return jnp.broadcast_to(jnp.sum(spread, axis=1, keepdims=True), (SLOTS, LANES)).astype(jnp.int32)


def faces_kernel(lengths, connect, orient, field, faces, held, slots, near, link, turn, sems):
    lane = iota(1)
    tiles = faces.shape[0] // 3
    pieces = [(c, pl.ds(h * PER_TILE, PER_TILE)) for c in range(3) for h in range(tiles)]
    small = [
        pltpu.make_async_copy(ref, to, sems.at[len(pieces) + k])
        for k, (ref, to) in enumerate(((lengths, near), (connect, link), (orient, turn)))
    ]
    copies = [pltpu.make_async_copy(field.at[at], held.at[at], sems.at[k]) for k, at in enumerate(pieces)]
    for copy in small + copies:
        copy.start()
    for copy in small:
        copy.wait()
    for k, ref in enumerate((near, link, turn)):
        slots[k] = by_slot(ref)
    source = slots[0] - HALO_LINES + jnp.minimum(lane % GROUP, HALO_LINES - 1)
    for k, copy in enumerate(copies):
        copy.wait()
        c, h = divmod(k, tiles)
        tile = jnp.zeros((SLOTS, LANES), jnp.float32)
        for j in range(PER_TILE):
            picked = jnp.take_along_axis(
                held[c, h * PER_TILE + j], source, axis=1, mode="promise_in_bounds"
            )
            tile = jnp.where(lane // GROUP == j, picked, tile)
        faces[k] = tile


def interior_kernel(begin, more, *refs):
    slots, project, band, field, stretch, *refs = refs
    before, (rates, coef, edge) = (refs[0] if more else None), refs[-3:]
    part = lax.axis_index("line")
    lane = iota(1)
    live = is_live(slots)
    scale = live * (1.0 / 180.0)
    sums = [[None] * 3 for _ in range(4)]
    for h in range(edge.shape[0]):
        tile = jnp.zeros((SLOTS, LANES), jnp.float32)
        at = begin + h * PER_TILE
        for j in range(PER_TILE):
            tile = jnp.where(lane // GROUP == j, pltpu.roll(stretch[at + j], GROUP * j, 1), tile)
        edge[h] = tile
        for c in range(3):
            block = field[c, at : at + PER_TILE] * live
            flat = block.reshape(PER_TILE * SLOTS, LANES)
            high = flat.astype(jnp.bfloat16)
            low = (flat - high.astype(jnp.float32)).astype(jnp.bfloat16)
            second = jnp.dot(
                jnp.concatenate([high, low], axis=1), band[...], preferred_element_type=jnp.float32
            ).reshape(PER_TILE, SLOTS, LANES)
            for j in range(PER_TILE):
                rate = (stretch[at + j] * scale) * second[j]
                rates[c, h * PER_TILE + j] = rate
                pre = block[j] + 0.1 * rate
                for r in range(4):
                    term = project[part, r, at + j : at + j + 1, :] * pre
                    sums[r][c] = term if sums[r][c] is None else sums[r][c] + term
    for r in range(4):
        for c in range(3):
            coef[r, c] = sums[r][c] + before[r, c] if more else sums[r][c]


def ghost_kernel(slots, packed, chip, far, pair, swap, edge_a, edge_b, coef, delta, near_out, far_out, far_too):
    part = lax.axis_index("line")
    blk = lax.axis_index("blk")
    count = lax.axis_size("blk")
    even = blk % 2 == 0
    lane = iota(1)
    tiles = chip.shape[0]
    parts = tiles // 3
    shift = (slots[1] // SLOTS - blk) & (count - 1)
    src = slots[1] % SLOTS
    is_one, is_two, is_three = shift == count // 2, shift == count // 2 + 1, shift == count // 2 + 2
    raw = []
    for k in range(tiles):
        pick = lambda v: jnp.take_along_axis(v, src, axis=0, mode="promise_in_bounds")
        row = pick(jnp.where(even, swap[k], chip[k]))
        row = jnp.where(is_one, pick(jnp.where(even, swap[2 * tiles + k], pair[k])), row)
        row = jnp.where(is_two, pick(jnp.where(even, swap[tiles + k], swap[k])), row)
        raw.append(jnp.where(is_three, pick(jnp.where(even, far[k], swap[tiles + k])), row))
    turn = slots[2]
    cosine = jnp.where(turn == 0, 1.0, jnp.where(turn == 2, -1.0, 0.0))
    sine = jnp.where(turn == 1, 1.0, jnp.where(turn == 3, -1.0, 0.0))
    at = lane % GROUP
    w0 = jnp.where(at < 3, STENCIL[0] / 180.0, 0.0)
    w1 = jnp.where(at < 2, STENCIL[1] / 180.0, 0.0)
    w2 = jnp.where(at < 1, STENCIL[2] / 180.0, 0.0)
    sums = [None] * 12
    for h in range(parts):
        g0 = cosine * raw[h] - sine * raw[parts + h]
        g1 = sine * raw[h] + cosine * raw[parts + h]
        for c, g in enumerate((g0, g1, raw[2 * parts + h])):
            second = w0 * g + w1 * pltpu.roll(g, LANES - 1, 1) + w2 * pltpu.roll(g, LANES - 2, 1)
            rate = (edge_a[h] if h < edge_a.shape[0] else edge_b[h - edge_a.shape[0]]) * second
            delta[c * parts + h] = rate
            for r in range(4):
                term = packed[part, r, h : h + 1, :] * rate
                i = 3 * r + c
                sums[i] = term if h == 0 else sums[i] + term
    for step in (GROUP, 2 * GROUP, 4 * GROUP, 8 * GROUP, 16 * GROUP):
        sums = [v + pltpu.roll(v, step, 1) for v in sums]
    first = jnp.where(lane < HALO_LINES, 0.1, 0.0)
    for r in range(4):
        for c in range(3):
            total = coef[r, c] + first * sums[3 * r + c]
            if r < 2:
                near_out[r, c] = total
            else:
                far_out[r - 2, c] = total
                far_too[r - 2, c] = total


def local_kernel(slots, forward, back, field, rates_a, rates_b, delta, rates, local, full, held, sems):
    part = lax.axis_index("line")
    size = field.shape[1]
    live = is_live(slots)
    first = iota(1) < HALO_LINES
    tiles = size // PER_TILE
    zero = jnp.zeros((SLOTS, LANES), jnp.float32)
    step = 8

    def advance(p, x, state):
        weight = [forward[part, k, pl.ds(p, 1), :] for k in range(5)]
        new = []
        for c in range(3):
            x2, x1, y1, y2 = state[c]
            y = (weight[0] * x2 + weight[1] * x1 + weight[2] * x[c] + weight[4] * y2) + weight[3] * y1
            held[c, p] = y
            new.append((x1, x[c], y, y1))
        return new

    state = [(zero, zero, zero, zero)] * 3
    copies = []
    for h in range(tiles):
        ghosts = [delta[c * tiles + h] for c in range(3)]
        inner, offset = (rates_a, 0) if h * PER_TILE < rates_a.shape[1] else (rates_b, rates_a.shape[1])

        def body(i, carry, h=h, inner=inner, offset=offset):
            state, ghosts = carry
            for u in range(step):
                p = h * PER_TILE + step * i + u
                x = []
                for c in range(3):
                    ghost = ghosts[c] if u == 0 else pltpu.roll(ghosts[c], LANES - GROUP * u, 1)
                    rate = inner[c, p - offset] + jnp.where(first, ghost, 0.0)
                    full[c, p] = rate
                    x.append(field[c, p] * live + 0.1 * rate)
                state = advance(p, x, state)
            return state, [pltpu.roll(g, LANES - GROUP * step, 1) for g in ghosts]

        state, _ = lax.fori_loop(0, PER_TILE // step, body, (state, ghosts))
        at = (slice(None), pl.ds(h * PER_TILE, PER_TILE))
        copies.append(pltpu.make_async_copy(full.at[at], rates.at[at], sems.at[h]))
        copies[-1].start()
    state = advance(size, [zero] * 3, state)

    def descend(i, carry):
        new = list(carry)
        for u in range(step):
            p = size - 1 - (step * i + u)
            one, two = back[part, 0, pl.ds(p, 1), :], back[part, 1, pl.ds(p, 1), :]
            for c in range(3):
                z1, z2 = new[c]
                z = (held[c, p + 1] + two * z2) + one * z1
                local[c, p] = z
                new[c] = (z, z1)
        return new

    lax.fori_loop(0, size // step, descend, [(zero, zero)] * 3)
    for copy in copies:
        copy.wait()


def last_kernel(outer, local, two, three, one, advanced, full, sems):
    part = lax.axis_index("line")
    size = local.shape[1]
    got = jnp.concatenate(
        [jnp.concatenate([ref[r, c] for c in range(3)], axis=1) for ref in (one, two, three) for r in range(2)], axis=0
    )
    high = got.astype(jnp.bfloat16)
    low = (got - high.astype(jnp.float32)).astype(jnp.bfloat16)
    got = jnp.concatenate([high, low, high], axis=0)
    copies = []
    for h in range(size // PER_TILE):
        rows = slice(h * PER_TILE * SLOTS, (h + 1) * PER_TILE * SLOTS)
        total = jnp.dot(outer[part, rows, :], got, preferred_element_type=jnp.float32)
        at = pl.ds(h * PER_TILE, PER_TILE)
        for c in range(3):
            tile = total[:, c * LANES : (c + 1) * LANES].reshape(PER_TILE, SLOTS, LANES)
            full[c, at] = local[c, at] + tile
            copies.append(pltpu.make_async_copy(full.at[c, at], advanced.at[c, at], sems.at[3 * h + c]))
            copies[-1].start()
    for copy in copies:
        copy.wait()


SMEM = pl.BlockSpec(memory_space=pltpu.SMEM)
VMEM = pl.BlockSpec(memory_space=pltpu.VMEM)
HBM = pl.BlockSpec(memory_space=pltpu.HBM)


def call(kernel, name, ins, outs, mib, flops, moved, scratch=(), out_specs=None, kinds={}):
    return pl.pallas_call(
        kernel,
        out_shape=[jax.ShapeDtypeStruct(s, kinds.get(k, jnp.float32)) for k, s in enumerate(outs)],
        in_specs=ins,
        out_specs=out_specs or [VMEM] * len(outs),
        scratch_shapes=scratch,
        compiler_params=pltpu.CompilerParams(vmem_limit_bytes=mib << 20),
        cost_estimate=pl.CostEstimate(flops=flops, bytes_accessed=moved, transcendentals=0),
        name=name,
    )


def shards(field, stretch, lengths, connect, orient, *, points, parts, count):
    size = field.shape[1]
    project, packed, forward, back, outer, band = (jnp.asarray(t) for t in tables(points, parts))
    tiles = 3 * (size // PER_TILE)
    block = (3, size, SLOTS, LANES)
    packed_tile = (tiles, SLOTS, LANES)
    sums = (4, 3, SLOTS, LANES)
    half = count // 2
    dma = pltpu.SemaphoreType.DMA

    def over_blk(x, pairs):
        return lax.ppermute(x, "blk", pairs)

    core = [(d ^ 1, d) for d in range(count)]
    pair = [(d if d % 2 == 0 else (d + half) % count, d) for d in range(count)]
    far = [((d + half + 2) % count if d % 2 == 0 else (d - 2) % count, d) for d in range(count)]

    lengths, connect, orient = (v[None] for v in (lengths, connect, orient))
    field, lengths, connect, orient = (
        pltpu.with_memory_space_constraint(v, pltpu.HBM) for v in (field, lengths, connect, orient)
    )
    with jax.named_scope("faces"):
        faces, held, slots = call(
            faces_kernel, "faces", [HBM] * 4, [packed_tile, block, (3, SLOTS, LANES)], 8, 10**6, 1200000,
            scratch=[pltpu.VMEM((1, SLOTS), jnp.int32)] * 3 + [dma((tiles + 3,))], kinds={2: jnp.int32},
        )(lengths, connect, orient, field)
        chip = over_blk(faces, core)

    def inside(begin, length, metric, *before):
        return call(
            functools.partial(interior_kernel, begin, bool(before)), "interior", [VMEM] * (5 + len(before)),
            [(3, length, SLOTS, LANES), sums, (length // PER_TILE, SLOTS, LANES)], 8, 10**7, 1500000,
        )(slots, project, band, held, metric, *before)

    with jax.named_scope("interior"):
        rates_a, coef, edge_a = inside(0, PER_TILE, stretch)
        chip, rates_a, coef, edge_a = lax.optimization_barrier((chip, rates_a, coef, edge_a))
    with jax.named_scope("faces"):
        both = jnp.concatenate([faces, chip], axis=0)
        from_far = over_blk(both, far)
        from_pair = over_blk(both, pair)
        from_far, coef = lax.optimization_barrier((from_far, coef))
        middle = jnp.where(lax.axis_index("blk") % 2 == 0, from_far[tiles:], from_pair[:tiles])
        swapped = over_blk(jnp.concatenate([from_far[:tiles], middle, from_pair[tiles:]], axis=0), core)
    with jax.named_scope("interior"):
        rates_b, coef, edge_b = inside(PER_TILE, size - PER_TILE, stretch, coef)
    with jax.named_scope("ghosts"):
        delta, near_sum, far_sum, far_again = call(
            ghost_kernel, "ghosts", [VMEM] * 9,
            [packed_tile] + [(2, 3, SLOTS, LANES)] * 3, 8, 10**6, 500000,
        )(slots, packed, chip, from_far, from_pair, swapped, edge_a, edge_b, coef)

    def over_line(x, k):
        return lax.ppermute(x, "line", [(e ^ k, e) for e in range(parts)])

    with jax.named_scope("line"):
        got = [over_line(near_sum, 1), over_line(far_sum, 2), over_line(far_again, 3)]
    with jax.named_scope("local"):
        rates, local = call(
            local_kernel, "local", [VMEM] * 7, [block, block], 12, 10**8, 6000000,
            out_specs=[HBM, VMEM],
            scratch=[
                pltpu.VMEM(block, jnp.float32),
                pltpu.VMEM((3, size + 1, SLOTS, LANES), jnp.float32),
                dma((size // PER_TILE,)),
            ],
        )(slots, forward, back, held, rates_a, rates_b, delta)
    with jax.named_scope("last"):
        (advanced,) = call(
            last_kernel, "last", [VMEM] * 5, [block], 8, 10**7, 2400000, out_specs=[HBM],
            scratch=[pltpu.VMEM(block, jnp.float32), dma((tiles,))],
        )(outer, local, got[1], got[2], got[0])
    return rates, advanced


def solution(mesh):
    parts, count = mesh.shape["line"], mesh.shape["blk"]

    def run(field, stretch, lengths, connect, orient):
        body = functools.partial(shards, points=field.shape[1], parts=parts, count=count)
        spec = P(None, "line", "blk", None)
        return jax.shard_map(
            body,
            mesh=mesh,
            in_specs=(spec, P("line", "blk", None), P("blk"), P("blk"), P("blk")),
            out_specs=(spec, spec),
            check_vma=False,
        )(field, stretch, lengths, connect, orient)

    return run
```

```python
import functools

import jax
import jax.numpy as jnp
import ml_dtypes
import numpy as np
from jax import lax
from jax.experimental import pallas as pl
from jax.experimental.pallas import tpu as pltpu
from jax.sharding import PartitionSpec as P

HALO_LINES = 3
STENCIL = (2.0, -27.0, 270.0, -490.0, 270.0, -27.0, 2.0)
SLOTS, LANES = 8, 128
GROUP = 4
PER_TILE = LANES // GROUP


def implicit_matrix(count):
    gap = np.abs(np.arange(count)[:, None] - np.arange(count)[None, :])
    amat = np.where(gap == 0, 1.0, 0.0) + np.where(gap == 1, 2.0 / 11.0, 0.0)
    bmat = (
        np.where(gap == 0, -24.0 / 11.0 - 3.0 / 22.0, 0.0)
        + np.where(gap == 1, 12.0 / 11.0, 0.0)
        + np.where(gap == 2, 3.0 / 44.0, 0.0)
    )
    inverse = np.linalg.inv(amat - 800.0 * bmat)
    return inverse, inverse @ amat


@functools.lru_cache(None)
def tables(count, parts):
    inverse, kmat = implicit_matrix(count)
    size = count // parts
    cut = [slice(e * size, (e + 1) * size) for e in range(parts)]
    basis = {}
    for e in range(parts):
        for side, rows in (("after", slice((e + 1) * size, count)), ("before", slice(0, e * size))):
            block = kmat[rows, cut[e]]
            if block.size:
                basis[e, side] = np.linalg.svd(block, full_matrices=False)[2][:2]
    side = lambda e, i: "after" if i > e else "before"
    project = np.zeros((parts, 4, size))
    out = np.zeros((parts, 6, size))
    for e in range(parts):
        assert side(e, e ^ 2) == side(e, e ^ 3)
        project[e, 0:2] = basis[e, side(e, e ^ 1)]
        project[e, 2:4] = basis[e, side(e, e ^ 2)]
        for k in (1, 2, 3):
            src = e ^ k
            out[e, 2 * k - 2 : 2 * k] = (kmat[cut[e], cut[src]] @ basis[src, side(src, e)].T).T
    packed = np.zeros((parts, 4, size // PER_TILE, LANES))
    for h in range(size // PER_TILE):
        packed[:, :, h] = np.repeat(project[:, :, h * PER_TILE : (h + 1) * PER_TILE], GROUP, axis=2)
    rows = lambda t: np.repeat(t[..., None], LANES, axis=-1).astype(np.float32)
    forward = np.zeros((parts, 5, size + SLOTS))
    back = np.zeros((parts, 2, size))
    for e, c in enumerate(cut):
        inner, lower, pivot, upper, right = own_block(kmat, inverse, c)
        for p in range(size):
            for k, q in enumerate((p - 1, p, p + 1)):
                if 0 <= q < size:
                    forward[e, k, p + 1] = right[p, q] / pivot[p]
            for k in (1, 2):
                if p >= k:
                    forward[e, 2 + k, p + 1] = -lower[p, p - k] * pivot[p - k] / pivot[p]
                if p + k < size:
                    back[e, k - 1, p] = -upper[p, p + k]
    outer = np.stack([np.kron(t.T, np.eye(SLOTS)) for t in out])
    high, low = split(outer)
    outer = np.concatenate([high, high, low], axis=2)
    line = np.arange(LANES)
    gap = line[:, None] - line[None, :] + 3
    band = np.where((gap >= 0) & (gap <= 6), np.take(np.asarray(STENCIL), np.clip(gap, 0, 6)), 0.0)
    band = np.concatenate([band, band]).astype(ml_dtypes.bfloat16)
    return rows(project), packed.astype(np.float32), rows(forward), rows(back), outer, band


def split(x):
    high = x.astype(ml_dtypes.bfloat16)
    return high, (x - high.astype(np.float64)).astype(ml_dtypes.bfloat16)


def own_block(kmat, inverse, c):
    t = np.linalg.inv(inverse[c, c])
    right = t @ kmat[c, c]
    size = len(t)
    gap = np.abs(np.arange(size)[:, None] - np.arange(size)[None, :])
    assert np.abs(t[gap > 2]).max() < 1e-8 and np.abs(right[gap > 1]).max() < 1e-8
    t = np.where(gap > 2, 0.0, t)
    upper = t.copy()
    lower = np.eye(size)
    for p in range(size):
        for q in range(p + 1, min(p + 3, size)):
            lower[q, p] = upper[q, p] / upper[p, p]
            upper[q] -= lower[q, p] * upper[p]
    pivot = np.diag(upper).copy()
    return t, lower, pivot, upper / pivot[:, None], right


def iota(axis):
    return lax.broadcasted_iota(jnp.int32, (SLOTS, LANES), axis)


def is_live(slots):
    return jnp.where(iota(1) < slots[...], 1.0, 0.0).astype(jnp.float32)


def by_slot(ref):
    shape = (SLOTS, SLOTS)
    own = lax.broadcasted_iota(jnp.int32, shape, 0) == lax.broadcasted_iota(jnp.int32, shape, 1)
    spread = jnp.where(own, jnp.broadcast_to(ref[...], shape).astype(jnp.float32), 0.0)
    return jnp.broadcast_to(jnp.sum(spread, axis=1, keepdims=True), (SLOTS, LANES)).astype(jnp.int32)


def faces_kernel(lengths, field, faces, held, slots, near, sems):
    lane = iota(1)
    tiles = faces.shape[0] // 3
    small = pltpu.make_async_copy(lengths, near, sems.at[3])
    copies = [pltpu.make_async_copy(field.at[c], held.at[c], sems.at[c]) for c in range(3)]
    small.start()
    for copy in copies:
        copy.start()
    small.wait()
    slots[...] = by_slot(near)
    source = slots[...] - HALO_LINES + jnp.minimum(lane % GROUP, HALO_LINES - 1)
    for c, copy in enumerate(copies):
        copy.wait()
        for h in range(tiles):
            tile = jnp.zeros((SLOTS, LANES), jnp.float32)
            for j in range(PER_TILE):
                picked = jnp.take_along_axis(
                    held[c, h * PER_TILE + j], source, axis=1, mode="promise_in_bounds"
                )
                tile = jnp.where(lane // GROUP == j, picked, tile)
            faces[c * tiles + h] = tile


def joins_kernel(connect, orient, joins, link, turn, sems):
    copies = [pltpu.make_async_copy(ref, to, sems.at[k]) for k, (ref, to) in enumerate(((connect, link), (orient, turn)))]
    for copy in copies:
        copy.start()
    for k, (copy, to) in enumerate(zip(copies, (link, turn))):
        copy.wait()
        joins[k] = by_slot(to)


def interior_kernel(begin, more, *refs):
    slots, project, band, field, stretch, *refs = refs
    before, (rates, coef, edge) = (refs[0] if more else None), refs[-3:]
    part = lax.axis_index("line")
    lane = iota(1)
    live = is_live(slots)
    scale = live * (1.0 / 180.0)
    sums = [[None] * 3 for _ in range(4)]
    for h in range(edge.shape[0]):
        tile = jnp.zeros((SLOTS, LANES), jnp.float32)
        at = begin + h * PER_TILE
        for j in range(PER_TILE):
            tile = jnp.where(lane // GROUP == j, pltpu.roll(stretch[at + j], GROUP * j, 1), tile)
        edge[h] = tile
        for c in range(3):
            block = field[c, at : at + PER_TILE] * live
            flat = block.reshape(PER_TILE * SLOTS, LANES)
            high = flat.astype(jnp.bfloat16)
            low = (flat - high.astype(jnp.float32)).astype(jnp.bfloat16)
            second = jnp.dot(
                jnp.concatenate([high, low], axis=1), band[...], preferred_element_type=jnp.float32
            ).reshape(PER_TILE, SLOTS, LANES)
            for j in range(PER_TILE):
                rate = (stretch[at + j] * scale) * second[j]
                rates[c, h * PER_TILE + j] = rate
                pre = block[j] + 0.1 * rate
                for r in range(4):
                    term = project[part, r, at + j : at + j + 1, :] * pre
                    sums[r][c] = term if sums[r][c] is None else sums[r][c] + term
    for r in range(4):
        for c in range(3):
            coef[r, c] = sums[r][c] + before[r, c] if more else sums[r][c]


def ghost_kernel(joins, packed, chip, far, pair, swap, edge_a, edge_b, coef, delta, near_out, far_out, far_too):
    part = lax.axis_index("line")
    blk = lax.axis_index("blk")
    count = lax.axis_size("blk")
    even = blk % 2 == 0
    lane = iota(1)
    tiles = chip.shape[0]
    parts = tiles // 3
    shift = (joins[0] // SLOTS - blk) & (count - 1)
    src = joins[0] % SLOTS
    is_one, is_two, is_three = shift == count // 2, shift == count // 2 + 1, shift == count // 2 + 2
    raw = []
    for k in range(tiles):
        pick = lambda v: jnp.take_along_axis(v, src, axis=0, mode="promise_in_bounds")
        row = pick(jnp.where(even, swap[k], chip[k]))
        row = jnp.where(is_one, pick(jnp.where(even, swap[2 * tiles + k], pair[k])), row)
        row = jnp.where(is_two, pick(jnp.where(even, swap[tiles + k], swap[k])), row)
        raw.append(jnp.where(is_three, pick(jnp.where(even, far[k], swap[tiles + k])), row))
    turn = joins[1]
    cosine = jnp.where(turn == 0, 1.0, jnp.where(turn == 2, -1.0, 0.0))
    sine = jnp.where(turn == 1, 1.0, jnp.where(turn == 3, -1.0, 0.0))
    at = lane % GROUP
    w0 = jnp.where(at < 3, STENCIL[0] / 180.0, 0.0)
    w1 = jnp.where(at < 2, STENCIL[1] / 180.0, 0.0)
    w2 = jnp.where(at < 1, STENCIL[2] / 180.0, 0.0)
    sums = [None] * 12
    for h in range(parts):
        g0 = cosine * raw[h] - sine * raw[parts + h]
        g1 = sine * raw[h] + cosine * raw[parts + h]
        for c, g in enumerate((g0, g1, raw[2 * parts + h])):
            second = w0 * g + w1 * pltpu.roll(g, LANES - 1, 1) + w2 * pltpu.roll(g, LANES - 2, 1)
            rate = (edge_a[h] if h < edge_a.shape[0] else edge_b[h - edge_a.shape[0]]) * second
            delta[c * parts + h] = rate
            for r in range(4):
                term = packed[part, r, h : h + 1, :] * rate
                i = 3 * r + c
                sums[i] = term if h == 0 else sums[i] + term
    for step in (GROUP, 2 * GROUP, 4 * GROUP, 8 * GROUP, 16 * GROUP):
        sums = [v + pltpu.roll(v, step, 1) for v in sums]
    first = jnp.where(lane < HALO_LINES, 0.1, 0.0)
    for r in range(4):
        for c in range(3):
            total = coef[r, c] + first * sums[3 * r + c]
            if r < 2:
                near_out[r, c] = total
            else:
                far_out[r - 2, c] = total
                far_too[r - 2, c] = total


def local_kernel(slots, forward, back, field, rates_a, rates_b, delta, rates, local, full, held, sems):
    part = lax.axis_index("line")
    size = field.shape[1]
    live = is_live(slots)
    first = iota(1) < HALO_LINES
    tiles = size // PER_TILE
    zero = jnp.zeros((SLOTS, LANES), jnp.float32)
    step = 8

    def advance(p, x, state):
        weight = [forward[part, k, pl.ds(p, 1), :] for k in range(5)]
        new = []
        for c in range(3):
            x2, x1, y1, y2 = state[c]
            y = (weight[0] * x2 + weight[1] * x1 + weight[2] * x[c] + weight[4] * y2) + weight[3] * y1
            held[c, p] = y
            new.append((x1, x[c], y, y1))
        return new

    state = [(zero, zero, zero, zero)] * 3
    copies = []
    for h in range(tiles):
        ghosts = [delta[c * tiles + h] for c in range(3)]
        inner, offset = (rates_a, 0) if h * PER_TILE < rates_a.shape[1] else (rates_b, rates_a.shape[1])

        def body(i, carry, h=h, inner=inner, offset=offset):
            state, ghosts = carry
            for u in range(step):
                p = h * PER_TILE + step * i + u
                x = []
                for c in range(3):
                    ghost = ghosts[c] if u == 0 else pltpu.roll(ghosts[c], LANES - GROUP * u, 1)
                    rate = inner[c, p - offset] + jnp.where(first, ghost, 0.0)
                    full[c, p] = rate
                    x.append(field[c, p] * live + 0.1 * rate)
                state = advance(p, x, state)
            return state, [pltpu.roll(g, LANES - GROUP * step, 1) for g in ghosts]

        state, _ = lax.fori_loop(0, PER_TILE // step, body, (state, ghosts))
        at = (slice(None), pl.ds(h * PER_TILE, PER_TILE))
        copies.append(pltpu.make_async_copy(full.at[at], rates.at[at], sems.at[h]))
        copies[-1].start()
    state = advance(size, [zero] * 3, state)

    def descend(i, carry):
        new = list(carry)
        for u in range(step):
            p = size - 1 - (step * i + u)
            one, two = back[part, 0, pl.ds(p, 1), :], back[part, 1, pl.ds(p, 1), :]
            for c in range(3):
                z1, z2 = new[c]
                z = (held[c, p + 1] + two * z2) + one * z1
                local[c, p] = z
                new[c] = (z, z1)
        return new

    lax.fori_loop(0, size // step, descend, [(zero, zero)] * 3)
    for copy in copies:
        copy.wait()


def last_kernel(outer, local, two, three, one, advanced, full, sems):
    part = lax.axis_index("line")
    size = local.shape[1]
    got = jnp.concatenate(
        [jnp.concatenate([ref[r, c] for c in range(3)], axis=1) for ref in (one, two, three) for r in range(2)], axis=0
    )
    high = got.astype(jnp.bfloat16)
    low = (got - high.astype(jnp.float32)).astype(jnp.bfloat16)
    got = jnp.concatenate([high, low, high], axis=0)
    copies = []
    for h in range(size // PER_TILE):
        rows = slice(h * PER_TILE * SLOTS, (h + 1) * PER_TILE * SLOTS)
        total = jnp.dot(outer[part, rows, :], got, preferred_element_type=jnp.float32)
        at = pl.ds(h * PER_TILE, PER_TILE)
        for c in range(3):
            tile = total[:, c * LANES : (c + 1) * LANES].reshape(PER_TILE, SLOTS, LANES)
            full[c, at] = local[c, at] + tile
        copies.append(pltpu.make_async_copy(full.at[:, at], advanced.at[:, at], sems.at[h]))
        copies[-1].start()
    for copy in copies:
        copy.wait()


SMEM = pl.BlockSpec(memory_space=pltpu.SMEM)
VMEM = pl.BlockSpec(memory_space=pltpu.VMEM)
HBM = pl.BlockSpec(memory_space=pltpu.HBM)


def call(kernel, name, ins, outs, mib, flops, moved, scratch=(), out_specs=None, kinds={}):
    return pl.pallas_call(
        kernel,
        out_shape=[jax.ShapeDtypeStruct(s, kinds.get(k, jnp.float32)) for k, s in enumerate(outs)],
        in_specs=ins,
        out_specs=out_specs or [VMEM] * len(outs),
        scratch_shapes=scratch,
        compiler_params=pltpu.CompilerParams(vmem_limit_bytes=mib << 20),
        cost_estimate=pl.CostEstimate(flops=flops, bytes_accessed=moved, transcendentals=0),
        name=name,
    )


def shards(field, stretch, lengths, connect, orient, *, points, parts, count):
    size = field.shape[1]
    project, packed, forward, back, outer, band = (jnp.asarray(t) for t in tables(points, parts))
    tiles = 3 * (size // PER_TILE)
    block = (3, size, SLOTS, LANES)
    packed_tile = (tiles, SLOTS, LANES)
    sums = (4, 3, SLOTS, LANES)
    half = count // 2
    dma = pltpu.SemaphoreType.DMA

    def over_blk(x, pairs):
        return lax.ppermute(x, "blk", pairs)

    core = [(d ^ 1, d) for d in range(count)]
    pair = [(d if d % 2 == 0 else (d + half) % count, d) for d in range(count)]
    far = [((d + half + 2) % count if d % 2 == 0 else (d - 2) % count, d) for d in range(count)]

    lengths, connect, orient = (v[None] for v in (lengths, connect, orient))
    field, lengths, connect, orient = (
        pltpu.with_memory_space_constraint(v, pltpu.HBM) for v in (field, lengths, connect, orient)
    )
    with jax.named_scope("faces"):
        faces, held, slots = call(
            faces_kernel, "faces", [HBM] * 2, [packed_tile, block, (SLOTS, LANES)], 8, 10**6, 1200000,
            scratch=[pltpu.VMEM((1, SLOTS), jnp.int32), dma((4,))], kinds={2: jnp.int32},
        )(lengths, field)
        chip = over_blk(faces, core)

    def inside(begin, length, metric, *before):
        return call(
            functools.partial(interior_kernel, begin, bool(before)), "interior", [VMEM] * (5 + len(before)),
            [(3, length, SLOTS, LANES), sums, (length // PER_TILE, SLOTS, LANES)], 8, 10**7, 1500000,
        )(slots, project, band, held, metric, *before)

    with jax.named_scope("interior"):
        rates_a, coef, edge_a = inside(0, PER_TILE, stretch)
        chip, rates_a, coef, edge_a = lax.optimization_barrier((chip, rates_a, coef, edge_a))
    with jax.named_scope("faces"):
        both = jnp.concatenate([faces, chip], axis=0)
        from_far = over_blk(both, far)
        from_pair = over_blk(both, pair)
        (joins,) = call(
            joins_kernel, "joins", [HBM] * 2, [(2, SLOTS, LANES)], 4, 10**5, 10**5,
            scratch=[pltpu.VMEM((1, SLOTS), jnp.int32)] * 2 + [dma((2,))], kinds={0: jnp.int32},
        )(*lax.optimization_barrier((connect, orient, chip))[:2])
        from_far, coef, joins = lax.optimization_barrier((from_far, coef, joins))
        middle = jnp.where(lax.axis_index("blk") % 2 == 0, from_far[tiles:], from_pair[:tiles])
        swapped = over_blk(jnp.concatenate([from_far[:tiles], middle, from_pair[tiles:]], axis=0), core)
    with jax.named_scope("interior"):
        rates_b, coef, edge_b = inside(PER_TILE, size - PER_TILE, stretch, coef)
    with jax.named_scope("ghosts"):
        delta, near_sum, far_sum, far_again = call(
            ghost_kernel, "ghosts", [VMEM] * 9,
            [packed_tile] + [(2, 3, SLOTS, LANES)] * 3, 8, 10**6, 500000,
        )(joins, packed, chip, from_far, from_pair, swapped, edge_a, edge_b, coef)

    def over_line(x, k):
        return lax.ppermute(x, "line", [(e ^ k, e) for e in range(parts)])

    with jax.named_scope("line"):
        got = [over_line(near_sum, 1), over_line(far_sum, 2), over_line(far_again, 3)]
    with jax.named_scope("local"):
        rates, local = call(
            local_kernel, "local", [VMEM] * 7, [block, block], 12, 10**8, 6000000,
            out_specs=[HBM, VMEM],
            scratch=[
                pltpu.VMEM(block, jnp.float32),
                pltpu.VMEM((3, size + 1, SLOTS, LANES), jnp.float32),
                dma((size // PER_TILE,)),
            ],
        )(slots, forward, back, held, rates_a, rates_b, delta)
    with jax.named_scope("last"):
        (advanced,) = call(
            last_kernel, "last", [VMEM] * 5, [block], 8, 10**7, 2400000, out_specs=[HBM],
            scratch=[pltpu.VMEM(block, jnp.float32), dma((size // PER_TILE,))],
        )(outer, local, got[1], got[2], got[0])
    return rates, advanced


def solution(mesh):
    parts, count = mesh.shape["line"], mesh.shape["blk"]

    def run(field, stretch, lengths, connect, orient):
        body = functools.partial(shards, points=field.shape[1], parts=parts, count=count)
        spec = P(None, "line", "blk", None)
        return jax.shard_map(
            body,
            mesh=mesh,
            in_specs=(spec, P("line", "blk", None), P("blk"), P("blk"), P("blk")),
            out_specs=(spec, spec),
            check_vma=False,
        )(field, stretch, lengths, connect, orient)

    return run
```

```python
import functools

import jax
import jax.numpy as jnp
import ml_dtypes
import numpy as np
from jax import lax
from jax.experimental import pallas as pl
from jax.experimental.pallas import tpu as pltpu
from jax.sharding import PartitionSpec as P

HALO_LINES = 3
STENCIL = (2.0, -27.0, 270.0, -490.0, 270.0, -27.0, 2.0)
SLOTS, LANES = 8, 128
GROUP = 4
PER_TILE = LANES // GROUP


def implicit_matrix(count):
    gap = np.abs(np.arange(count)[:, None] - np.arange(count)[None, :])
    amat = np.where(gap == 0, 1.0, 0.0) + np.where(gap == 1, 2.0 / 11.0, 0.0)
    bmat = (
        np.where(gap == 0, -24.0 / 11.0 - 3.0 / 22.0, 0.0)
        + np.where(gap == 1, 12.0 / 11.0, 0.0)
        + np.where(gap == 2, 3.0 / 44.0, 0.0)
    )
    inverse = np.linalg.inv(amat - 800.0 * bmat)
    return inverse, inverse @ amat


@functools.lru_cache(None)
def tables(count, parts):
    inverse, kmat = implicit_matrix(count)
    size = count // parts
    cut = [slice(e * size, (e + 1) * size) for e in range(parts)]
    basis = {}
    for e in range(parts):
        for side, rows in (("after", slice((e + 1) * size, count)), ("before", slice(0, e * size))):
            block = kmat[rows, cut[e]]
            if block.size:
                basis[e, side] = np.linalg.svd(block, full_matrices=False)[2][:2]
    side = lambda e, i: "after" if i > e else "before"
    project = np.zeros((parts, 4, size))
    out = np.zeros((parts, 6, size))
    for e in range(parts):
        assert side(e, e ^ 2) == side(e, e ^ 3)
        project[e, 0:2] = basis[e, side(e, e ^ 1)]
        project[e, 2:4] = basis[e, side(e, e ^ 2)]
        for k in (1, 2, 3):
            src = e ^ k
            out[e, 2 * k - 2 : 2 * k] = (kmat[cut[e], cut[src]] @ basis[src, side(src, e)].T).T
    packed = np.zeros((parts, 4, size // PER_TILE, LANES))
    for h in range(size // PER_TILE):
        packed[:, :, h] = np.repeat(project[:, :, h * PER_TILE : (h + 1) * PER_TILE], GROUP, axis=2)
    rows = lambda t: np.repeat(t[..., None], LANES, axis=-1).astype(np.float32)
    forward = np.zeros((parts, 5, size + SLOTS))
    back = np.zeros((parts, 2, size))
    for e, c in enumerate(cut):
        inner, lower, pivot, upper, right = own_block(kmat, inverse, c)
        for p in range(size):
            for k, q in enumerate((p - 1, p, p + 1)):
                if 0 <= q < size:
                    forward[e, k, p + 1] = right[p, q] / pivot[p]
            for k in (1, 2):
                if p >= k:
                    forward[e, 2 + k, p + 1] = -lower[p, p - k] * pivot[p - k] / pivot[p]
                if p + k < size:
                    back[e, k - 1, p] = -upper[p, p + k]
    outer = np.stack([np.kron(t.T, np.eye(SLOTS)) for t in out])
    high, low = split(outer)
    outer = np.concatenate([high, high, low], axis=2)
    line = np.arange(LANES)
    gap = line[:, None] - line[None, :] + 3
    band = np.where((gap >= 0) & (gap <= 6), np.take(np.asarray(STENCIL), np.clip(gap, 0, 6)), 0.0)
    band = np.concatenate([band, band]).astype(ml_dtypes.bfloat16)
    return rows(project), packed.astype(np.float32), rows(forward), rows(back), outer, band


def split(x):
    high = x.astype(ml_dtypes.bfloat16)
    return high, (x - high.astype(np.float64)).astype(ml_dtypes.bfloat16)


def own_block(kmat, inverse, c):
    t = np.linalg.inv(inverse[c, c])
    right = t @ kmat[c, c]
    size = len(t)
    gap = np.abs(np.arange(size)[:, None] - np.arange(size)[None, :])
    assert np.abs(t[gap > 2]).max() < 1e-8 and np.abs(right[gap > 1]).max() < 1e-8
    t = np.where(gap > 2, 0.0, t)
    upper = t.copy()
    lower = np.eye(size)
    for p in range(size):
        for q in range(p + 1, min(p + 3, size)):
            lower[q, p] = upper[q, p] / upper[p, p]
            upper[q] -= lower[q, p] * upper[p]
    pivot = np.diag(upper).copy()
    return t, lower, pivot, upper / pivot[:, None], right


def iota(axis):
    return lax.broadcasted_iota(jnp.int32, (SLOTS, LANES), axis)


def is_live(slots):
    return jnp.where(iota(1) < slots[...], 1.0, 0.0).astype(jnp.float32)


def by_slot(ref):
    shape = (SLOTS, SLOTS)
    own = lax.broadcasted_iota(jnp.int32, shape, 0) == lax.broadcasted_iota(jnp.int32, shape, 1)
    spread = jnp.where(own, jnp.broadcast_to(ref[...], shape).astype(jnp.float32), 0.0)
    return jnp.broadcast_to(jnp.sum(spread, axis=1, keepdims=True), (SLOTS, LANES)).astype(jnp.int32)


def faces_kernel(lengths, field, faces, held, slots, near, sems):
    lane = iota(1)
    tiles = faces.shape[0] // 3
    small = pltpu.make_async_copy(lengths, near, sems.at[3])
    copies = [pltpu.make_async_copy(field.at[c], held.at[c], sems.at[c]) for c in range(3)]
    small.start()
    for copy in copies:
        copy.start()
    small.wait()
    slots[...] = by_slot(near)
    source = slots[...] - HALO_LINES + jnp.minimum(lane % GROUP, HALO_LINES - 1)
    for c, copy in enumerate(copies):
        copy.wait()
        for h in range(tiles):
            tile = jnp.zeros((SLOTS, LANES), jnp.float32)
            for j in range(PER_TILE):
                picked = jnp.take_along_axis(
                    held[c, h * PER_TILE + j], source, axis=1, mode="promise_in_bounds"
                )
                tile = jnp.where(lane // GROUP == j, picked, tile)
            faces[c * tiles + h] = tile


def joins_kernel(connect, orient, joins, link, turn, sems):
    copies = [pltpu.make_async_copy(ref, to, sems.at[k]) for k, (ref, to) in enumerate(((connect, link), (orient, turn)))]
    for copy in copies:
        copy.start()
    for k, (copy, to) in enumerate(zip(copies, (link, turn))):
        copy.wait()
        joins[k] = by_slot(to)


def interior_kernel(begin, more, *refs):
    slots, project, band, field, stretch, *refs = refs
    before, (rates, coef, edge) = (refs[0] if more else None), refs[-3:]
    part = lax.axis_index("line")
    lane = iota(1)
    live = is_live(slots)
    scale = live * (1.0 / 180.0)
    sums = [[None] * 3 for _ in range(4)]
    for h in range(edge.shape[0]):
        tile = jnp.zeros((SLOTS, LANES), jnp.float32)
        at = begin + h * PER_TILE
        for j in range(PER_TILE):
            tile = jnp.where(lane // GROUP == j, pltpu.roll(stretch[at + j], GROUP * j, 1), tile)
        edge[h] = tile
        for c in range(3):
            block = field[c, at : at + PER_TILE] * live
            flat = block.reshape(PER_TILE * SLOTS, LANES)
            high = flat.astype(jnp.bfloat16)
            low = (flat - high.astype(jnp.float32)).astype(jnp.bfloat16)
            second = jnp.dot(
                jnp.concatenate([high, low], axis=1), band[...], preferred_element_type=jnp.float32
            ).reshape(PER_TILE, SLOTS, LANES)
            for j in range(PER_TILE):
                rate = (stretch[at + j] * scale) * second[j]
                rates[c, h * PER_TILE + j] = rate
                pre = block[j] + 0.1 * rate
                for r in range(4):
                    term = project[part, r, at + j : at + j + 1, :] * pre
                    sums[r][c] = term if sums[r][c] is None else sums[r][c] + term
    for r in range(4):
        for c in range(3):
            coef[r, c] = sums[r][c] + before[r, c] if more else sums[r][c]


def ghost_kernel(ring, joins, packed, other, swap, edge_a, edge_b, coef, delta, near_out, far_out, far_too):
    part = lax.axis_index("line")
    blk = lax.axis_index("blk")
    count = lax.axis_size("blk")
    even = blk % 2 == 0
    lane = iota(1)
    tiles = ring.shape[0]
    parts = tiles // 3
    shift = (joins[0] // SLOTS - blk) & (count - 1)
    src = joins[0] % SLOTS
    is_one, is_two, is_three = shift == count // 2, shift == count // 2 + 1, shift == count // 2 + 2
    raw = []
    for k in range(tiles):
        pick = lambda v: jnp.take_along_axis(v, src, axis=0, mode="promise_in_bounds")
        row = pick(ring[k])
        row = jnp.where(is_one, pick(jnp.where(even, other[k], swap[k])), row)
        row = jnp.where(is_two, pick(other[tiles + k]), row)
        raw.append(jnp.where(is_three, pick(jnp.where(even, swap[k], other[k])), row))
    turn = joins[1]
    cosine = jnp.where(turn == 0, 1.0, jnp.where(turn == 2, -1.0, 0.0))
    sine = jnp.where(turn == 1, 1.0, jnp.where(turn == 3, -1.0, 0.0))
    at = lane % GROUP
    w0 = jnp.where(at < 3, STENCIL[0] / 180.0, 0.0)
    w1 = jnp.where(at < 2, STENCIL[1] / 180.0, 0.0)
    w2 = jnp.where(at < 1, STENCIL[2] / 180.0, 0.0)
    sums = [None] * 12
    for h in range(parts):
        g0 = cosine * raw[h] - sine * raw[parts + h]
        g1 = sine * raw[h] + cosine * raw[parts + h]
        for c, g in enumerate((g0, g1, raw[2 * parts + h])):
            second = w0 * g + w1 * pltpu.roll(g, LANES - 1, 1) + w2 * pltpu.roll(g, LANES - 2, 1)
            rate = (edge_a[h] if h < edge_a.shape[0] else edge_b[h - edge_a.shape[0]]) * second
            delta[c * parts + h] = rate
            for r in range(4):
                term = packed[part, r, h : h + 1, :] * rate
                i = 3 * r + c
                sums[i] = term if h == 0 else sums[i] + term
    for step in (GROUP, 2 * GROUP, 4 * GROUP, 8 * GROUP, 16 * GROUP):
        sums = [v + pltpu.roll(v, step, 1) for v in sums]
    first = jnp.where(lane < HALO_LINES, 0.1, 0.0)
    for r in range(4):
        for c in range(3):
            total = coef[r, c] + first * sums[3 * r + c]
            if r < 2:
                near_out[r, c] = total
            else:
                far_out[r - 2, c] = total
                far_too[r - 2, c] = total


def local_kernel(slots, forward, back, field, rates_a, rates_b, delta, rates, local, full, held, sems):
    part = lax.axis_index("line")
    size = field.shape[1]
    live = is_live(slots)
    first = iota(1) < HALO_LINES
    tiles = size // PER_TILE
    zero = jnp.zeros((SLOTS, LANES), jnp.float32)
    step = 8

    def advance(p, x, state):
        weight = [forward[part, k, pl.ds(p, 1), :] for k in range(5)]
        new = []
        for c in range(3):
            x2, x1, y1, y2 = state[c]
            y = (weight[0] * x2 + weight[1] * x1 + weight[2] * x[c] + weight[4] * y2) + weight[3] * y1
            held[c, p] = y
            new.append((x1, x[c], y, y1))
        return new

    state = [(zero, zero, zero, zero)] * 3
    copies = []
    for h in range(tiles):
        ghosts = [delta[c * tiles + h] for c in range(3)]
        inner, offset = (rates_a, 0) if h * PER_TILE < rates_a.shape[1] else (rates_b, rates_a.shape[1])

        def body(i, carry, h=h, inner=inner, offset=offset):
            state, ghosts = carry
            for u in range(step):
                p = h * PER_TILE + step * i + u
                x = []
                for c in range(3):
                    ghost = ghosts[c] if u == 0 else pltpu.roll(ghosts[c], LANES - GROUP * u, 1)
                    rate = inner[c, p - offset] + jnp.where(first, ghost, 0.0)
                    full[c, p] = rate
                    x.append(field[c, p] * live + 0.1 * rate)
                state = advance(p, x, state)
            return state, [pltpu.roll(g, LANES - GROUP * step, 1) for g in ghosts]

        state, _ = lax.fori_loop(0, PER_TILE // step, body, (state, ghosts))
        at = (slice(None), pl.ds(h * PER_TILE, PER_TILE))
        copies.append(pltpu.make_async_copy(full.at[at], rates.at[at], sems.at[h]))
        copies[-1].start()
    state = advance(size, [zero] * 3, state)

    def descend(i, carry):
        new = list(carry)
        for u in range(step):
            p = size - 1 - (step * i + u)
            one, two = back[part, 0, pl.ds(p, 1), :], back[part, 1, pl.ds(p, 1), :]
            for c in range(3):
                z1, z2 = new[c]
                z = (held[c, p + 1] + two * z2) + one * z1
                local[c, p] = z
                new[c] = (z, z1)
        return new

    lax.fori_loop(0, size // step, descend, [(zero, zero)] * 3)
    for copy in copies:
        copy.wait()


def last_kernel(outer, local, two, three, one, advanced, full, sems):
    part = lax.axis_index("line")
    size = local.shape[1]
    got = jnp.concatenate(
        [jnp.concatenate([ref[r, c] for c in range(3)], axis=1) for ref in (one, two, three) for r in range(2)], axis=0
    )
    high = got.astype(jnp.bfloat16)
    low = (got - high.astype(jnp.float32)).astype(jnp.bfloat16)
    got = jnp.concatenate([high, low, high], axis=0)
    copies = []
    for h in range(size // PER_TILE):
        rows = slice(h * PER_TILE * SLOTS, (h + 1) * PER_TILE * SLOTS)
        total = jnp.dot(outer[part, rows, :], got, preferred_element_type=jnp.float32)
        at = pl.ds(h * PER_TILE, PER_TILE)
        for c in range(3):
            tile = total[:, c * LANES : (c + 1) * LANES].reshape(PER_TILE, SLOTS, LANES)
            full[c, at] = local[c, at] + tile
        copies.append(pltpu.make_async_copy(full.at[:, at], advanced.at[:, at], sems.at[h]))
        copies[-1].start()
    for copy in copies:
        copy.wait()


SMEM = pl.BlockSpec(memory_space=pltpu.SMEM)
VMEM = pl.BlockSpec(memory_space=pltpu.VMEM)
HBM = pl.BlockSpec(memory_space=pltpu.HBM)


def call(kernel, name, ins, outs, mib, flops, moved, scratch=(), out_specs=None, kinds={}):
    return pl.pallas_call(
        kernel,
        out_shape=[jax.ShapeDtypeStruct(s, kinds.get(k, jnp.float32)) for k, s in enumerate(outs)],
        in_specs=ins,
        out_specs=out_specs or [VMEM] * len(outs),
        scratch_shapes=scratch,
        compiler_params=pltpu.CompilerParams(vmem_limit_bytes=mib << 20),
        cost_estimate=pl.CostEstimate(flops=flops, bytes_accessed=moved, transcendentals=0),
        name=name,
    )


def shards(field, stretch, lengths, connect, orient, *, points, parts, count):
    size = field.shape[1]
    project, packed, forward, back, outer, band = (jnp.asarray(t) for t in tables(points, parts))
    tiles = 3 * (size // PER_TILE)
    block = (3, size, SLOTS, LANES)
    packed_tile = (tiles, SLOTS, LANES)
    sums = (4, 3, SLOTS, LANES)
    half = count // 2
    dma = pltpu.SemaphoreType.DMA

    def over_blk(x, pairs):
        return lax.ppermute(x, "blk", pairs)

    core = [(d ^ 1, d) for d in range(count)]
    ring = [((d - 1) % count, d) for d in range(count)]
    other = [((d + half + 2 * (d % 2)) % count, d) for d in range(count)]

    lengths, connect, orient = (v[None] for v in (lengths, connect, orient))
    field, lengths, connect, orient = (
        pltpu.with_memory_space_constraint(v, pltpu.HBM) for v in (field, lengths, connect, orient)
    )
    with jax.named_scope("faces"):
        faces, held, slots = call(
            faces_kernel, "faces", [HBM] * 2, [packed_tile, block, (SLOTS, LANES)], 8, 10**6, 1200000,
            scratch=[pltpu.VMEM((1, SLOTS), jnp.int32), dma((4,))], kinds={2: jnp.int32},
        )(lengths, field)
        chip = over_blk(faces, core)
        before = over_blk(faces, ring)

    def inside(begin, length, metric, *before):
        return call(
            functools.partial(interior_kernel, begin, bool(before)), "interior", [VMEM] * (5 + len(before)),
            [(3, length, SLOTS, LANES), sums, (length // PER_TILE, SLOTS, LANES)], 8, 10**7, 1500000,
        )(slots, project, band, held, metric, *before)

    with jax.named_scope("interior"):
        rates_a, coef, edge_a = inside(0, PER_TILE, stretch)
    with jax.named_scope("faces"):
        both = jnp.concatenate([faces, chip], axis=0)
        from_other = over_blk(both, other)
        (joins,) = call(
            joins_kernel, "joins", [HBM] * 2, [(2, SLOTS, LANES)], 4, 10**5, 10**5,
            scratch=[pltpu.VMEM((1, SLOTS), jnp.int32)] * 2 + [dma((2,))], kinds={0: jnp.int32},
        )(*lax.optimization_barrier((connect, orient, chip))[:2])
        from_other, coef, joins, rates_a, edge_a = lax.optimization_barrier((from_other, coef, joins, rates_a, edge_a))
        swapped = over_blk(from_other[tiles:], core)
    with jax.named_scope("interior"):
        rates_b, coef, edge_b = inside(PER_TILE, size - PER_TILE, stretch, coef)
    with jax.named_scope("ghosts"):
        delta, near_sum, far_sum, far_again = call(
            ghost_kernel, "ghosts", [VMEM] * 8,
            [packed_tile] + [(2, 3, SLOTS, LANES)] * 3, 8, 10**6, 500000,
        )(before, joins, packed, from_other, swapped, edge_a, edge_b, coef)

    def over_line(x, k):
        return lax.ppermute(x, "line", [(e ^ k, e) for e in range(parts)])

    with jax.named_scope("line"):
        got = [over_line(near_sum, 1), over_line(far_sum, 2), over_line(far_again, 3)]
    with jax.named_scope("local"):
        rates, local = call(
            local_kernel, "local", [VMEM] * 7, [block, block], 12, 10**8, 6000000,
            out_specs=[HBM, VMEM],
            scratch=[
                pltpu.VMEM(block, jnp.float32),
                pltpu.VMEM((3, size + 1, SLOTS, LANES), jnp.float32),
                dma((size // PER_TILE,)),
            ],
        )(slots, forward, back, held, rates_a, rates_b, delta)
    with jax.named_scope("last"):
        (advanced,) = call(
            last_kernel, "last", [VMEM] * 5, [block], 8, 10**7, 2400000, out_specs=[HBM],
            scratch=[pltpu.VMEM(block, jnp.float32), dma((size // PER_TILE,))],
        )(outer, local, got[1], got[2], got[0])
    return rates, advanced


def solution(mesh):
    parts, count = mesh.shape["line"], mesh.shape["blk"]

    def run(field, stretch, lengths, connect, orient):
        body = functools.partial(shards, points=field.shape[1], parts=parts, count=count)
        spec = P(None, "line", "blk", None)
        return jax.shard_map(
            body,
            mesh=mesh,
            in_specs=(spec, P("line", "blk", None), P("blk"), P("blk"), P("blk")),
            out_specs=(spec, spec),
            check_vma=False,
        )(field, stretch, lengths, connect, orient)

    return run
```

```python
import functools

import jax
import jax.numpy as jnp
import ml_dtypes
import numpy as np
from jax import lax
from jax.experimental import pallas as pl
from jax.experimental.pallas import tpu as pltpu
from jax.sharding import PartitionSpec as P

HALO_LINES = 3
STENCIL = (2.0, -27.0, 270.0, -490.0, 270.0, -27.0, 2.0)
SLOTS, LANES = 8, 128
GROUP = 4
PER_TILE = LANES // GROUP


def implicit_matrix(count):
    gap = np.abs(np.arange(count)[:, None] - np.arange(count)[None, :])
    amat = np.where(gap == 0, 1.0, 0.0) + np.where(gap == 1, 2.0 / 11.0, 0.0)
    bmat = (
        np.where(gap == 0, -24.0 / 11.0 - 3.0 / 22.0, 0.0)
        + np.where(gap == 1, 12.0 / 11.0, 0.0)
        + np.where(gap == 2, 3.0 / 44.0, 0.0)
    )
    inverse = np.linalg.inv(amat - 800.0 * bmat)
    return inverse, inverse @ amat


@functools.lru_cache(None)
def tables(count, parts):
    inverse, kmat = implicit_matrix(count)
    size = count // parts
    cut = [slice(e * size, (e + 1) * size) for e in range(parts)]
    basis = {}
    for e in range(parts):
        for side, rows in (("after", slice((e + 1) * size, count)), ("before", slice(0, e * size))):
            block = kmat[rows, cut[e]]
            if block.size:
                basis[e, side] = np.linalg.svd(block, full_matrices=False)[2][:2]
    side = lambda e, i: "after" if i > e else "before"
    project = np.zeros((parts, 4, size))
    out = np.zeros((parts, 6, size))
    for e in range(parts):
        assert side(e, e ^ 2) == side(e, e ^ 3)
        project[e, 0:2] = basis[e, side(e, e ^ 1)]
        project[e, 2:4] = basis[e, side(e, e ^ 2)]
        for k in (1, 2, 3):
            src = e ^ k
            out[e, 2 * k - 2 : 2 * k] = (kmat[cut[e], cut[src]] @ basis[src, side(src, e)].T).T
    packed = np.zeros((parts, 4, size // PER_TILE, LANES))
    for h in range(size // PER_TILE):
        packed[:, :, h] = np.repeat(project[:, :, h * PER_TILE : (h + 1) * PER_TILE], GROUP, axis=2)
    rows = lambda t: np.repeat(t[..., None], LANES, axis=-1).astype(np.float32)
    forward = np.zeros((parts, 5, size + SLOTS))
    back = np.zeros((parts, 2, size))
    for e, c in enumerate(cut):
        inner, lower, pivot, upper, right = own_block(kmat, inverse, c)
        for p in range(size):
            for k, q in enumerate((p - 1, p, p + 1)):
                if 0 <= q < size:
                    forward[e, k, p + 1] = right[p, q] / pivot[p]
            for k in (1, 2):
                if p >= k:
                    forward[e, 2 + k, p + 1] = -lower[p, p - k] * pivot[p - k] / pivot[p]
                if p + k < size:
                    back[e, k - 1, p] = -upper[p, p + k]
    outer = np.stack([np.kron(t.T, np.eye(SLOTS)) for t in out])
    high, low = split(outer)
    outer = np.concatenate([high, high, low], axis=2)
    line = np.arange(LANES)
    gap = line[:, None] - line[None, :] + 3
    band = np.where((gap >= 0) & (gap <= 6), np.take(np.asarray(STENCIL), np.clip(gap, 0, 6)), 0.0)
    band = np.concatenate([band, band]).astype(ml_dtypes.bfloat16)
    return rows(project), packed.astype(np.float32), rows(forward), rows(back), outer, band


def split(x):
    high = x.astype(ml_dtypes.bfloat16)
    return high, (x - high.astype(np.float64)).astype(ml_dtypes.bfloat16)


def own_block(kmat, inverse, c):
    t = np.linalg.inv(inverse[c, c])
    right = t @ kmat[c, c]
    size = len(t)
    gap = np.abs(np.arange(size)[:, None] - np.arange(size)[None, :])
    assert np.abs(t[gap > 2]).max() < 1e-8 and np.abs(right[gap > 1]).max() < 1e-8
    t = np.where(gap > 2, 0.0, t)
    upper = t.copy()
    lower = np.eye(size)
    for p in range(size):
        for q in range(p + 1, min(p + 3, size)):
            lower[q, p] = upper[q, p] / upper[p, p]
            upper[q] -= lower[q, p] * upper[p]
    pivot = np.diag(upper).copy()
    return t, lower, pivot, upper / pivot[:, None], right


def iota(axis):
    return lax.broadcasted_iota(jnp.int32, (SLOTS, LANES), axis)


def is_live(slots):
    return jnp.where(iota(1) < slots[...], 1.0, 0.0).astype(jnp.float32)


def by_slot(ref):
    shape = (SLOTS, SLOTS)
    own = lax.broadcasted_iota(jnp.int32, shape, 0) == lax.broadcasted_iota(jnp.int32, shape, 1)
    spread = jnp.where(own, jnp.broadcast_to(ref[...], shape).astype(jnp.float32), 0.0)
    return jnp.broadcast_to(jnp.sum(spread, axis=1, keepdims=True), (SLOTS, LANES)).astype(jnp.int32)


def faces_kernel(lengths, field, faces, held, slots, near, sems):
    lane = iota(1)
    tiles = faces.shape[0] // 3
    small = pltpu.make_async_copy(lengths, near, sems.at[3])
    copies = [pltpu.make_async_copy(field.at[c], held.at[c], sems.at[c]) for c in range(3)]
    small.start()
    for copy in copies:
        copy.start()
    small.wait()
    slots[...] = by_slot(near)
    source = slots[...] - HALO_LINES + jnp.minimum(lane % GROUP, HALO_LINES - 1)
    for c, copy in enumerate(copies):
        copy.wait()
        for h in range(tiles):
            tile = jnp.zeros((SLOTS, LANES), jnp.float32)
            for j in range(PER_TILE):
                picked = jnp.take_along_axis(
                    held[c, h * PER_TILE + j], source, axis=1, mode="promise_in_bounds"
                )
                tile = jnp.where(lane // GROUP == j, picked, tile)
            faces[c * tiles + h] = tile


def joins_kernel(connect, orient, joins, link, turn, sems):
    copies = [pltpu.make_async_copy(ref, to, sems.at[k]) for k, (ref, to) in enumerate(((connect, link), (orient, turn)))]
    for copy in copies:
        copy.start()
    for k, (copy, to) in enumerate(zip(copies, (link, turn))):
        copy.wait()
        joins[k] = by_slot(to)


def interior_kernel(begin, more, *refs):
    slots, project, band, field, stretch, *refs = refs
    before, (rates, coef, edge) = (refs[0] if more else None), refs[-3:]
    part = lax.axis_index("line")
    lane = iota(1)
    live = is_live(slots)
    scale = live * (1.0 / 180.0)
    sums = [[None] * 3 for _ in range(4)]
    for h in range(edge.shape[0]):
        tile = jnp.zeros((SLOTS, LANES), jnp.float32)
        at = begin + h * PER_TILE
        for j in range(PER_TILE):
            tile = jnp.where(lane // GROUP == j, pltpu.roll(stretch[at + j], GROUP * j, 1), tile)
        edge[h] = tile
        for c in range(3):
            block = field[c, at : at + PER_TILE] * live
            flat = block.reshape(PER_TILE * SLOTS, LANES)
            high = flat.astype(jnp.bfloat16)
            low = (flat - high.astype(jnp.float32)).astype(jnp.bfloat16)
            second = jnp.dot(
                jnp.concatenate([high, low], axis=1), band[...], preferred_element_type=jnp.float32
            ).reshape(PER_TILE, SLOTS, LANES)
            for j in range(PER_TILE):
                rate = (stretch[at + j] * scale) * second[j]
                rates[c, h * PER_TILE + j] = rate
                pre = block[j] + 0.1 * rate
                for r in range(4):
                    term = project[part, r, at + j : at + j + 1, :] * pre
                    sums[r][c] = term if sums[r][c] is None else sums[r][c] + term
    for r in range(4):
        for c in range(3):
            coef[r, c] = sums[r][c] + before[r, c] if more else sums[r][c]


def ghost_kernel(ring, joins, packed, other, swap, edge_a, edge_b, coef, delta, near_out, far_out, far_too):
    part = lax.axis_index("line")
    blk = lax.axis_index("blk")
    count = lax.axis_size("blk")
    even = blk % 2 == 0
    lane = iota(1)
    tiles = ring.shape[0]
    parts = tiles // 3
    shift = (joins[0] // SLOTS - blk) & (count - 1)
    src = joins[0] % SLOTS
    is_one, is_two, is_three = shift == count // 2, shift == count // 2 + 1, shift == count // 2 + 2
    raw = []
    for k in range(tiles):
        pick = lambda v: jnp.take_along_axis(v, src, axis=0, mode="promise_in_bounds")
        row = pick(ring[k])
        row = jnp.where(is_one, pick(jnp.where(even, other[k], swap[k])), row)
        row = jnp.where(is_two, pick(other[tiles + k]), row)
        raw.append(jnp.where(is_three, pick(jnp.where(even, swap[k], other[k])), row))
    turn = joins[1]
    cosine = jnp.where(turn == 0, 1.0, jnp.where(turn == 2, -1.0, 0.0))
    sine = jnp.where(turn == 1, 1.0, jnp.where(turn == 3, -1.0, 0.0))
    at = lane % GROUP
    w0 = jnp.where(at < 3, STENCIL[0] / 180.0, 0.0)
    w1 = jnp.where(at < 2, STENCIL[1] / 180.0, 0.0)
    w2 = jnp.where(at < 1, STENCIL[2] / 180.0, 0.0)
    sums = [None] * 12
    for h in range(parts):
        g0 = cosine * raw[h] - sine * raw[parts + h]
        g1 = sine * raw[h] + cosine * raw[parts + h]
        for c, g in enumerate((g0, g1, raw[2 * parts + h])):
            second = w0 * g + w1 * pltpu.roll(g, LANES - 1, 1) + w2 * pltpu.roll(g, LANES - 2, 1)
            rate = (edge_a[h] if h < edge_a.shape[0] else edge_b[h - edge_a.shape[0]]) * second
            delta[c * parts + h] = rate
            for r in range(4):
                term = packed[part, r, h : h + 1, :] * rate
                i = 3 * r + c
                sums[i] = term if h == 0 else sums[i] + term
    for step in (GROUP, 2 * GROUP, 4 * GROUP, 8 * GROUP, 16 * GROUP):
        sums = [v + pltpu.roll(v, step, 1) for v in sums]
    first = jnp.where(lane < HALO_LINES, 0.1, 0.0)
    for r in range(4):
        for c in range(3):
            total = coef[r, c] + first * sums[3 * r + c]
            if r < 2:
                near_out[r, c] = total
            else:
                far_out[r - 2, c] = total
                far_too[r - 2, c] = total


def local_kernel(slots, forward, back, field, rates_a, rates_b, delta, rates, local, full, held, sems):
    part = lax.axis_index("line")
    size = field.shape[1]
    live = is_live(slots)
    first = iota(1) < HALO_LINES
    tiles = size // PER_TILE
    zero = jnp.zeros((SLOTS, LANES), jnp.float32)
    step = 8

    def advance(p, x, state):
        weight = [forward[part, k, pl.ds(p, 1), :] for k in range(5)]
        new = []
        for c in range(3):
            x2, x1, y1, y2 = state[c]
            y = (weight[0] * x2 + weight[1] * x1 + weight[2] * x[c] + weight[4] * y2) + weight[3] * y1
            held[c, p] = y
            new.append((x1, x[c], y, y1))
        return new

    state = [(zero, zero, zero, zero)] * 3
    copies = []
    for h in range(tiles):
        ghosts = [delta[c * tiles + h] for c in range(3)]
        inner, offset = (rates_a, 0) if h * PER_TILE < rates_a.shape[1] else (rates_b, rates_a.shape[1])

        def body(i, carry, h=h, inner=inner, offset=offset):
            state, ghosts = carry
            for u in range(step):
                p = h * PER_TILE + step * i + u
                x = []
                for c in range(3):
                    ghost = ghosts[c] if u == 0 else pltpu.roll(ghosts[c], LANES - GROUP * u, 1)
                    rate = inner[c, p - offset] + jnp.where(first, ghost, 0.0)
                    full[c, p] = rate
                    x.append(field[c, p] * live + 0.1 * rate)
                state = advance(p, x, state)
            return state, [pltpu.roll(g, LANES - GROUP * step, 1) for g in ghosts]

        state, _ = lax.fori_loop(0, PER_TILE // step, body, (state, ghosts))
        at = (slice(None), pl.ds(h * PER_TILE, PER_TILE))
        copies.append(pltpu.make_async_copy(full.at[at], rates.at[at], sems.at[h]))
        copies[-1].start()
    state = advance(size, [zero] * 3, state)

    def descend(i, carry):
        new = list(carry)
        for u in range(step):
            p = size - 1 - (step * i + u)
            one, two = back[part, 0, pl.ds(p, 1), :], back[part, 1, pl.ds(p, 1), :]
            for c in range(3):
                z1, z2 = new[c]
                z = (held[c, p + 1] + two * z2) + one * z1
                local[c, p] = z
                new[c] = (z, z1)
        return new

    lax.fori_loop(0, size // step, descend, [(zero, zero)] * 3)
    for copy in copies:
        copy.wait()


def last_kernel(outer, local, two, three, one, advanced, full, sems):
    part = lax.axis_index("line")
    size = local.shape[1]
    got = jnp.concatenate(
        [jnp.concatenate([ref[r, c] for c in range(3)], axis=1) for ref in (one, two, three) for r in range(2)], axis=0
    )
    high = got.astype(jnp.bfloat16)
    low = (got - high.astype(jnp.float32)).astype(jnp.bfloat16)
    got = jnp.concatenate([high, low, high], axis=0)
    copies = []
    for h in range(size // PER_TILE):
        rows = slice(h * PER_TILE * SLOTS, (h + 1) * PER_TILE * SLOTS)
        total = jnp.dot(outer[part, rows, :], got, preferred_element_type=jnp.float32)
        at = pl.ds(h * PER_TILE, PER_TILE)
        for c in range(3):
            tile = total[:, c * LANES : (c + 1) * LANES].reshape(PER_TILE, SLOTS, LANES)
            full[c, at] = local[c, at] + tile
        copies.append(pltpu.make_async_copy(full.at[:, at], advanced.at[:, at], sems.at[h]))
        copies[-1].start()
    for copy in copies:
        copy.wait()


SMEM = pl.BlockSpec(memory_space=pltpu.SMEM)
VMEM = pl.BlockSpec(memory_space=pltpu.VMEM)
HBM = pl.BlockSpec(memory_space=pltpu.HBM)


def call(kernel, name, ins, outs, mib, flops, moved, scratch=(), out_specs=None, kinds={}):
    return pl.pallas_call(
        kernel,
        out_shape=[jax.ShapeDtypeStruct(s, kinds.get(k, jnp.float32)) for k, s in enumerate(outs)],
        in_specs=ins,
        out_specs=out_specs or [VMEM] * len(outs),
        scratch_shapes=scratch,
        compiler_params=pltpu.CompilerParams(vmem_limit_bytes=mib << 20),
        cost_estimate=pl.CostEstimate(flops=flops, bytes_accessed=moved, transcendentals=0),
        name=name,
    )


def shards(field, stretch, lengths, connect, orient, *, points, parts, count):
    size = field.shape[1]
    project, packed, forward, back, outer, band = (jnp.asarray(t) for t in tables(points, parts))
    tiles = 3 * (size // PER_TILE)
    block = (3, size, SLOTS, LANES)
    packed_tile = (tiles, SLOTS, LANES)
    sums = (4, 3, SLOTS, LANES)
    half = count // 2
    dma = pltpu.SemaphoreType.DMA

    def over_blk(x, pairs):
        return lax.ppermute(x, "blk", pairs)

    core = [(d ^ 1, d) for d in range(count)]
    ring = [((d - 1) % count, d) for d in range(count)]
    other = [((d + half + 2 * (d % 2)) % count, d) for d in range(count)]

    lengths, connect, orient = (v[None] for v in (lengths, connect, orient))
    field, lengths, connect, orient = (
        pltpu.with_memory_space_constraint(v, pltpu.HBM) for v in (field, lengths, connect, orient)
    )
    with jax.named_scope("faces"):
        faces, held, slots = call(
            faces_kernel, "faces", [HBM] * 2, [packed_tile, block, (SLOTS, LANES)], 8, 10**6, 1200000,
            scratch=[pltpu.VMEM((1, SLOTS), jnp.int32), dma((4,))], kinds={2: jnp.int32},
        )(lengths, field)
        chip = over_blk(faces, core)
        before = over_blk(faces, ring)

    def inside(begin, length, metric, *before):
        return call(
            functools.partial(interior_kernel, begin, bool(before)), "interior", [VMEM] * (5 + len(before)),
            [(3, length, SLOTS, LANES), sums, (length // PER_TILE, SLOTS, LANES)], 8, 10**7, 1500000,
        )(slots, project, band, held, metric, *before)

    with jax.named_scope("interior"):
        rates_a, coef, edge_a = inside(0, PER_TILE, stretch)
    with jax.named_scope("faces"):
        (joins,) = call(
            joins_kernel, "joins", [HBM] * 2, [(2, SLOTS, LANES)], 4, 10**5, 10**5,
            scratch=[pltpu.VMEM((1, SLOTS), jnp.int32)] * 2 + [dma((2,))], kinds={0: jnp.int32},
        )(connect, orient)
        chip, joins = lax.optimization_barrier((chip, joins))
        both = jnp.concatenate([faces, chip], axis=0)
        from_other = over_blk(both, other)
        from_other, coef, rates_a, edge_a = lax.optimization_barrier((from_other, coef, rates_a, edge_a))
        swapped = over_blk(from_other[tiles:], core)
    with jax.named_scope("interior"):
        rates_b, coef, edge_b = inside(PER_TILE, size - PER_TILE, stretch, coef)
    with jax.named_scope("ghosts"):
        delta, near_sum, far_sum, far_again = call(
            ghost_kernel, "ghosts", [VMEM] * 8,
            [packed_tile] + [(2, 3, SLOTS, LANES)] * 3, 8, 10**6, 500000,
        )(before, joins, packed, from_other, swapped, edge_a, edge_b, coef)

    def over_line(x, k):
        return lax.ppermute(x, "line", [(e ^ k, e) for e in range(parts)])

    with jax.named_scope("line"):
        got = [over_line(near_sum, 1), over_line(far_sum, 2), over_line(far_again, 3)]
    with jax.named_scope("local"):
        rates, local = call(
            local_kernel, "local", [VMEM] * 7, [block, block], 12, 10**8, 6000000,
            out_specs=[HBM, VMEM],
            scratch=[
                pltpu.VMEM(block, jnp.float32),
                pltpu.VMEM((3, size + 1, SLOTS, LANES), jnp.float32),
                dma((size // PER_TILE,)),
            ],
        )(slots, forward, back, held, rates_a, rates_b, delta)
    with jax.named_scope("last"):
        (advanced,) = call(
            last_kernel, "last", [VMEM] * 5, [block], 8, 10**7, 2400000, out_specs=[HBM],
            scratch=[pltpu.VMEM(block, jnp.float32), dma((size // PER_TILE,))],
        )(outer, local, got[1], got[2], got[0])
    return rates, advanced


def solution(mesh):
    parts, count = mesh.shape["line"], mesh.shape["blk"]

    def run(field, stretch, lengths, connect, orient):
        body = functools.partial(shards, points=field.shape[1], parts=parts, count=count)
        spec = P(None, "line", "blk", None)
        return jax.shard_map(
            body,
            mesh=mesh,
            in_specs=(spec, P("line", "blk", None), P("blk"), P("blk"), P("blk")),
            out_specs=(spec, spec),
            check_vma=False,
        )(field, stretch, lengths, connect, orient)

    return run
```
